128 devices in a mesh: band: 32 (over z, y, core), face: 4 (over x).
Axes of the slice: x: 4, y: 4, z: 4, core: 2. Of those that a mesh axis runs over, the one named last changes fastest.
Arguments:
- grid_feat: bfloat16 [262144, 227], P(('band', 'face')), may hold values from -6 to 6
- mesh_nodes: bfloat16 [65536, 512], P(('band', 'face')), may hold values from -6 to 6
- g2m_sender: int32 [128, 2048], P(('band', 'face')), may hold values from 0 to 2047, as said below
- g2m_receiver: int32 [128, 2048], P(('band', 'face')), may hold values from 0 to 511
- send_counts: int32 [128, 128], P(('band', 'face')), may hold values from 4 to 16, as said below
- edge_sender: int32 [128, 4096], P(('band', 'face')), may hold values from 0 to 1535
- edge_receiver: int32 [128, 4096], P(('band', 'face')), may hold values from 0 to 511
- embed_in: bfloat16 [227, 512], replicated, may hold values from -0.375 to 0.375
- embed_out: bfloat16 [512, 512], replicated, may hold values from -0.25 to 0.25
- proj_grid: bfloat16 [512, 512], replicated, may hold values from -0.25 to 0.25
- proj_mesh: bfloat16 [512, 512], replicated, may hold values from -0.25 to 0.25
- node_self: bfloat16 [512, 512], replicated, may hold values from -0.25 to 0.25
- node_agg: bfloat16 [512, 512], replicated, may hold values from -0.25 to 0.25
- edge_send: bfloat16 [512, 512], replicated, may hold values from -0.25 to 0.25
- edge_recv: bfloat16 [512, 512], replicated, may hold values from -0.25 to 0.25
- out_self: bfloat16 [512, 512], replicated, may hold values from -0.25 to 0.25
- out_agg: bfloat16 [512, 512], replicated, may hold values from -0.25 to 0.25
Outputs:
- mesh_out: float32 [65536, 512], P(('band', 'face'))
The draws below stay inside these ranges and needn't reach their ends.
Inputs may be any that keep to these rules, and one draw needn't show every extreme that they name: `send_counts`: entry [i, o]: the first that many of the 16 slots from device i to owner o are live. In every draw some owner receives 16 from every device. `g2m_sender`: A row of the sending device's own grid rows; among the 16 slots from one device to one owner no row repeats. `g2m_receiver`: A row of the owner's mesh rows. `edge_sender`: see the steps for its meaning. `edge_receiver`: A row of the device's own mesh rows.
All inputs are finite; a program needn't handle non-finite values.
Results may differ from the reference program's by a relative error of at most 0.008.
Values may be sent and summed in bfloat16 or wider, within the bound.
No kernel may reach another device: no remote copies, remote signals or barrier semaphores. Data moves between devices by JAX's collectives and lax.ppermute only.
A program may use at most 64 MiB of HBM per device.

```python
import jax
import jax.numpy as jnp
from jax import lax

F = 227
L = 512
G_DEV = 2048
SLOT_DEV = 2048
MESH_DEV = 512
OWNERS = 128
ME_DEV = 4096
GRID = 262144
MESH = 65536
N_BAND = 32
N_FACE = 4


def draw_send_counts(key, part):
    key = jax.random.fold_in(key, 7)
    base_key = jax.random.fold_in(key, 1)
    full_key = jax.random.fold_in(key, 2)
    cap = SLOT_DEV // OWNERS
    base = jax.random.randint(base_key, (OWNERS, OWNERS), cap // 4, cap // 2 + 1)
    owner = jnp.arange(OWNERS, dtype=jnp.int32)[None, :]
    device = jnp.arange(OWNERS, dtype=jnp.int32)[:, None]
    near = jnp.abs(owner // N_FACE - device // N_FACE) <= 1
    rim = max(OWNERS // 32, 1)
    polar = (owner < rim) | (owner >= OWNERS - rim)
    counts = jnp.where(near | polar, cap, base)
    full_owner = jax.random.randint(full_key, (), 0, OWNERS)
    counts = jnp.where(owner == full_owner, cap, counts)
    return counts.astype(jnp.int32)


def draw_g2m_sender(key, part):
    key = jax.random.fold_in(key, 11)
    perm_keys = jax.random.split(jax.random.fold_in(key, 1), OWNERS)
    perms = jax.vmap(lambda k: jax.random.permutation(k, G_DEV))(perm_keys).astype(jnp.int32)
    rounds = SLOT_DEV // G_DEV
    shifts = jax.random.randint(jax.random.fold_in(key, 2), (OWNERS, rounds), 0, G_DEV)
    slot = jnp.arange(SLOT_DEV, dtype=jnp.int32)
    position = (slot[None, :] + jnp.repeat(shifts, G_DEV, axis=1)) % G_DEV
    return jnp.take_along_axis(perms, position.astype(jnp.int32), axis=1).astype(jnp.int32)


def touch_ends(values, rng, least, largest):
    extent = values.shape
    place = [jax.random.randint(jax.random.fold_in(rng, axis), (), 0, extent[axis]) for axis in range(len(extent))]
    values = values.at[tuple(place)].set(least)
    longest = extent.index(max(extent))
    place[longest] = (place[longest] + 1) % extent[longest]
    return values.at[tuple(place)].set(largest)


def levels(own_key, shape, pieces, least, largest):
    def one(axis_at, blocks):
        draws = jax.random.uniform(jax.random.fold_in(jax.random.fold_in(own_key, 6), axis_at), (blocks,), jnp.float32, least / len(pieces), largest / len(pieces))
        return jnp.repeat(jnp.exp(draws), shape[axis_at] // blocks).reshape((-1,) + (1,) * (len(shape) - axis_at - 1))

    gain = one(*pieces[0])
    for cut in pieces[1:]:
        gain = gain * one(*cut)
    return gain


def noise(rng, shape, width, limit, pieces=(), kind=jnp.bfloat16):
    entries = jax.random.normal(rng, shape, jnp.float32) * width
    if len(pieces) > 0:
        entries = levels(rng, shape, pieces, -0.22, 0.18) * entries
    return jnp.clip(entries, min=-limit, max=limit).astype(kind)


def setup_inputs(seed: int = 0) -> dict:
    arg_keys = jax.random.split(jax.random.key(seed), 18)
    grid_feat = noise(arg_keys[0], (GRID, F), 1.0, 6.0, ((0, 128),))
    mesh_nodes = noise(arg_keys[1], (MESH, L), 1.0, 6.0, ((0, 128),))
    g2m_sender = draw_g2m_sender(jax.random.fold_in(arg_keys[17], 71), 0)
    g2m_receiver = touch_ends(jax.random.randint(arg_keys[3], (OWNERS, SLOT_DEV), 0, MESH_DEV), jax.random.fold_in(arg_keys[3], 1), 0, MESH_DEV - 1).astype(jnp.int32)
    send_counts = draw_send_counts(jax.random.fold_in(arg_keys[17], 71), 0)
    edge_sender = touch_ends(jax.random.randint(arg_keys[5], (OWNERS, ME_DEV), 0, 3 * MESH_DEV), jax.random.fold_in(arg_keys[5], 1), 0, (3 * MESH_DEV) - 1).astype(jnp.int32)
    edge_receiver = touch_ends(jax.random.randint(arg_keys[6], (OWNERS, ME_DEV), 0, MESH_DEV), jax.random.fold_in(arg_keys[6], 1), 0, MESH_DEV - 1).astype(jnp.int32)
    embed_in = noise(arg_keys[7], (F, L), F ** -0.5, 0.375)
    embed_out = noise(arg_keys[8], (L, L), L ** -0.5, 0.25)
    proj_grid = noise(arg_keys[9], (L, L), L ** -0.5, 0.25)
    proj_mesh = noise(arg_keys[10], (L, L), L ** -0.5, 0.25)
    node_self = noise(arg_keys[11], (L, L), L ** -0.5, 0.25)
    node_agg = noise(arg_keys[12], (L, L), L ** -0.5, 0.25)
    edge_send = noise(arg_keys[13], (L, L), L ** -0.5, 0.25)
    edge_recv = noise(arg_keys[14], (L, L), L ** -0.5, 0.25)
    out_self = noise(arg_keys[15], (L, L), L ** -0.5, 0.25)
    out_agg = noise(arg_keys[16], (L, L), L ** -0.5, 0.25)
    return dict(grid_feat=grid_feat, mesh_nodes=mesh_nodes, g2m_sender=g2m_sender, g2m_receiver=g2m_receiver, send_counts=send_counts, edge_sender=edge_sender, edge_receiver=edge_receiver, embed_in=embed_in, embed_out=embed_out, proj_grid=proj_grid, proj_mesh=proj_mesh, node_self=node_self, node_agg=node_agg, edge_send=edge_send, edge_recv=edge_recv, out_self=out_self, out_agg=out_agg)


def layer_norm(values):
    mean = lax.optimization_barrier(jnp.mean(values, axis=-1, keepdims=True))
    centered = values - mean
    variance = lax.optimization_barrier(jnp.mean(centered * centered, axis=-1, keepdims=True))
    return centered * lax.rsqrt(variance + 1e-05)

def reference(grid_feat, mesh_nodes, g2m_sender, g2m_receiver, send_counts, edge_sender, edge_receiver, embed_in, embed_out, proj_grid, proj_mesh, node_self, node_agg, edge_send, edge_recv, out_self, out_agg):
    owners = N_BAND * N_FACE
    cap = SLOT_DEV // owners
    mesh_proj = jnp.dot(mesh_nodes, proj_mesh, preferred_element_type=jnp.float32)
    feats = grid_feat.reshape(owners, G_DEV, F)
    slot = jnp.arange(SLOT_DEV, dtype=jnp.int32)
    owner_of = slot // cap
    within = slot % cap

    def step(total, item):
        feat, senders, receivers, counts = item
        hidden = jax.nn.silu(jnp.dot(feat, embed_in, preferred_element_type=jnp.float32)).astype(jnp.bfloat16)
        latent = jnp.dot(hidden, embed_out, preferred_element_type=jnp.float32).astype(jnp.bfloat16)
        proj = jnp.dot(latent, proj_grid, preferred_element_type=jnp.float32).astype(jnp.bfloat16)
        live = within < counts[owner_of]
        target = (owner_of * MESH_DEV + receivers).astype(jnp.int32)
        message = jax.nn.silu(proj[senders].astype(jnp.float32) + mesh_proj[target]).astype(jnp.bfloat16)
        target = jnp.where(live, target, owners * MESH_DEV).astype(jnp.int32)
        summed = jax.ops.segment_sum(message.astype(jnp.float32), target, num_segments=owners * MESH_DEV + 1)
        return (total + summed[:-1], None)
    start = jnp.zeros((owners * MESH_DEV, L), jnp.float32)
    gathered, _ = lax.scan(step, start, (feats, g2m_sender, g2m_receiver, send_counts))
    gathered = gathered.astype(jnp.bfloat16)
    inner = jnp.dot(mesh_nodes, node_self, preferred_element_type=jnp.float32) + jnp.dot(gathered, node_agg, preferred_element_type=jnp.float32)
    mesh_mid = (mesh_nodes.astype(jnp.float32) + jax.nn.silu(inner)).astype(jnp.bfloat16)
    send_proj = jnp.dot(mesh_mid, edge_send, preferred_element_type=jnp.float32)
    recv_proj = jnp.dot(mesh_mid, edge_recv, preferred_element_type=jnp.float32)
    blocks = send_proj.reshape(N_BAND, N_FACE, MESH_DEV, L)
    window = jnp.concatenate([jnp.roll(blocks, 1, axis=1), blocks, jnp.roll(blocks, -1, axis=1)], axis=2)
    window = window.reshape(owners, 3 * MESH_DEV, L)
    recv_blocks = recv_proj.reshape(owners, MESH_DEV, L)

    def local_layer(item):
        win, own, senders, receivers = item
        edge_msg = jax.nn.silu(win[senders] + own[receivers]).astype(jnp.bfloat16)
        return jax.ops.segment_sum(edge_msg.astype(jnp.float32), receivers, num_segments=MESH_DEV)
    mesh_sum = lax.map(local_layer, (window, recv_blocks, edge_sender, edge_receiver))
    mesh_sum = mesh_sum.reshape(owners * MESH_DEV, L).astype(jnp.bfloat16)
    update = jnp.dot(mesh_mid, out_self, preferred_element_type=jnp.float32) + jnp.dot(mesh_sum, out_agg, preferred_element_type=jnp.float32)
    return layer_norm(mesh_mid.astype(jnp.float32) + jax.nn.silu(update))
```

```python
import functools

import jax
import jax.numpy as jnp
from jax import lax
from jax.experimental import pallas as pl
from jax.experimental.pallas import tpu as pltpu
from jax.sharding import PartitionSpec as P

BF16 = jnp.bfloat16
F32 = jnp.float32
I32 = jnp.int32
WIDE = 256
SLOTS = 256
EDGES = 512
BLOCKS = 3
FEW = 256
SPAN = 256
ALIGN = 16
VMEM_BYTES = 40 * 1024 * 1024


def dot(a, b):
    return jnp.dot(a, b, preferred_element_type=F32)


def dot_rows(a, b):
    return lax.dot_general(a, b, (((1,), (1,)), ((), ())), preferred_element_type=F32)


def silu(v):
    half = 0.5 * v
    return half + half * jnp.tanh(half)


def one_hot(hit):
    return jnp.where(hit, 1.0, 0.0).astype(BF16)


def iota(shape, dim):
    return lax.broadcasted_iota(I32, shape, dim)


def as_column(row):
    return jnp.broadcast_to(row, (8, row.shape[1])).T[:, 0:1]


def part(ref, index):
    rows = ref.shape[1]
    return ref.at[index * rows : (index + 1) * rows, :]


def start_copies(pairs, sems):
    copies = [
        pltpu.make_async_copy(source, target, sems.at[i]) for i, (source, target) in enumerate(pairs)
    ]
    for copy in copies:
        copy.start()
    return copies


def call(kernel, outs, hbm, vmem, scratch=(), out_specs=None):
    there = pl.BlockSpec(memory_space=pltpu.HBM)
    here = pl.BlockSpec(memory_space=pltpu.VMEM)
    if out_specs is None:
        out_specs = jax.tree.map(lambda _: here, outs)
    args = [pltpu.with_memory_space_constraint(arg, pltpu.HBM) for arg in hbm]
    args += [pltpu.with_memory_space_constraint(arg, pltpu.VMEM) for arg in vmem]
    return pl.pallas_call(
        kernel,
        out_shape=outs,
        in_specs=[there] * len(hbm) + [here] * len(vmem),
        out_specs=out_specs,
        scratch_shapes=list(scratch),
        compiler_params=pltpu.CompilerParams(vmem_limit_bytes=VMEM_BYTES),
    )(*args)


def pack_kernel(
    mesh_rows,
    feat_hbm,
    sender_hbm,
    receiver_hbm,
    count_hbm,
    from_hbm,
    to_hbm,
    out_hbm,
    key_hbm,
    feat_ref,
    sender_ref,
    receiver_ref,
    count_ref,
    from_ref,
    to_ref,
    out_ref,
    key_ref,
    in_sem,
    feat_sem,
    out_sem,
    key_sem,
):
    feats, rows = feat_ref.shape
    slots = sender_ref.shape[1]
    owners = count_ref.shape[1]
    cap = slots // owners
    half = mesh_rows // 2
    small = start_copies(
        (
            (sender_hbm, sender_ref),
            (receiver_hbm, receiver_ref),
            (count_hbm, count_ref),
            (from_hbm, from_ref),
            (to_hbm, to_ref),
        ),
        in_sem,
    )
    pieces = feat_sem.shape[0]
    piece = rows // pieces
    cuts = [slice(i * piece, (i + 1) * piece) for i in range(pieces)]
    large = start_copies([(feat_hbm.at[:, cut], feat_ref.at[:, cut]) for cut in cuts], feat_sem)
    for copy in small:
        copy.wait()
    source = from_ref[...]
    row = lax.rem(source, mesh_rows)
    second = row // half
    mine = (source >= mesh_rows) & (source < 2 * mesh_rows)
    side = jnp.where(source < mesh_rows, half, 0)
    part = jnp.where(mine, 0, 1 + second)
    place = jnp.where(mine, row, row - second * half + side)
    key_ref[...] = (part * mesh_rows + to_ref[...]) * mesh_rows + place
    key_copy = pltpu.make_async_copy(key_ref, key_hbm, key_sem)
    key_copy.start()
    counts = jnp.broadcast_to(count_ref[...].astype(F32).astype(BF16), (8, owners))
    for copy in large:
        copy.wait()
    feat = feat_ref[...]
    outs = []
    for block, start in enumerate(range(0, slots, SLOTS)):
        here = slice(start, start + SLOTS)
        slot = iota((owners, SLOTS), 1) + start
        owner = iota((owners, SLOTS), 0)
        within_owner = (slot >= owner * cap) & (slot < owner * cap + cap)
        count = dot(counts, one_hot(within_owner)).astype(I32)
        lane = iota((8, SLOTS), 1) + start
        live = lax.rem(lane, cap) < count
        receiver = jnp.broadcast_to(receiver_ref[:, here], (8, SLOTS))
        sender = jnp.broadcast_to(sender_ref[:, here], (8, SLOTS))
        high = jnp.where(live, receiver >> 5, -1)
        low = jnp.where(live, receiver & 31, 0)
        line = iota((8, SLOTS), 0)
        columns = jnp.where(line == 0, sender, jnp.where(line == 1, high, low)).T
        picker = one_hot(columns[:, 0:1] == iota((SLOTS, rows), 1))
        column = iota((SLOTS, WIDE), 1)
        digits = jnp.where(
            column == feats, columns[:, 1:2], jnp.where(column == feats + 1, columns[:, 2:3], 0)
        )
        out_ref[here, :] = digits.astype(F32).astype(BF16)
        out_ref[here, :feats] = dot_rows(picker, feat).astype(BF16)
        copy = pltpu.make_async_copy(out_ref.at[here, :], out_hbm.at[here, :], out_sem.at[block])
        copy.start()
        outs.append(copy)
    for copy in outs:
        copy.wait()
    key_copy.wait()


def weights_kernel(
    embed_out_hbm,
    proj_grid_hbm,
    mesh_hbm,
    proj_mesh_hbm,
    node_self_hbm,
    key_hbm,
    fold_ref,
    proj_ref,
    self_ref,
    key_ref,
    embed_out_ref,
    proj_grid_ref,
    mesh_ref,
    proj_mesh_ref,
    node_self_ref,
    sems,
):
    pairs = (
        (embed_out_hbm, embed_out_ref),
        (proj_grid_hbm, proj_grid_ref),
        (mesh_hbm, mesh_ref),
        (proj_mesh_hbm, proj_mesh_ref),
        (node_self_hbm, node_self_ref),
        (key_hbm, key_ref),
    )
    copies = start_copies(pairs, sems)
    for copy in copies:
        copy.wait()
    fold_ref[...] = dot(embed_out_ref[...], proj_grid_ref[...]).astype(BF16)
    mesh = mesh_ref[...]
    proj_ref[...] = dot(mesh, proj_mesh_ref[...]).astype(BF16)
    self_ref[...] = dot(mesh, node_self_ref[...])


def gather_kernel(
    feats,
    mesh_hbm,
    node_agg_hbm,
    edge_send_hbm,
    edge_recv_hbm,
    out_self_hbm,
    out_agg_hbm,
    x_ref,
    embed_ref,
    fold_ref,
    proj_ref,
    self_ref,
    low_ref,
    high_ref,
    weight_ref,
    msg_ref,
    mesh_ref,
    node_agg_ref,
    sems,
):
    pairs = (
        (mesh_hbm, mesh_ref),
        (node_agg_hbm, node_agg_ref),
        (edge_send_hbm, part(weight_ref, 0)),
        (edge_recv_hbm, part(weight_ref, 1)),
        (out_self_hbm, part(weight_ref, 2)),
        (out_agg_hbm, part(weight_ref, 3)),
    )
    copies = start_copies(pairs, sems)
    slots = x_ref.shape[0]
    mesh_rows = mesh_ref.shape[0]
    half = mesh_rows // 2
    embed = embed_ref[...]
    fold = fold_ref[...]
    proj = proj_ref[...]

    def weight(place):
        return jnp.where(place == feats, 32.0, jnp.where(place == feats + 1, 1.0, 0.0)).astype(BF16)

    across = weight(iota((WIDE, 128), 0))
    along = weight(iota((8, WIDE), 1))
    targets = []
    for start in range(0, slots, SLOTS):
        here = slice(start, start + SLOTS)
        x = x_ref[here, :]
        hidden = silu(dot(x, embed)).astype(BF16)
        target = dot(x, across).astype(I32)[:, 0:1]
        picker = one_hot(target == iota((SLOTS, mesh_rows), 1))
        msg_ref[here, :] = silu(dot(hidden, fold) + dot(picker, proj)).astype(BF16)
        targets.append(dot_rows(along, x))
    target = jnp.concatenate(targets, axis=1).astype(I32)[0:1, :]
    for copy in copies:
        copy.wait()
    node_agg = node_agg_ref[...]
    for start, out_ref in ((0, low_ref), (half, high_ref)):
        here = slice(start, start + half)
        selector = one_hot(target == iota((half, slots), 0) + start)
        gathered = dot(selector, msg_ref[...]).astype(BF16)
        inner = self_ref[here, :] + dot(gathered, node_agg)
        out_ref[...] = (mesh_ref[here, :].astype(F32) + silu(inner)).astype(BF16)


def fetch_keys(key_in_ref, key_ref, key_scalar, sem):
    edges = key_in_ref.shape[1]
    copy = pltpu.make_async_copy(key_in_ref, key_scalar, sem)
    copy.start()
    key_ref[:, :edges] = key_in_ref[...]
    key_ref[:, edges:] = jnp.full((1, key_ref.shape[1] - edges), -1, I32)
    return copy


def edge_sums(part, key_scalar, key_ref, table_ref, recv_ref, acc_ref):
    mesh_rows = table_ref.shape[0]
    edges = key_scalar.shape[1]

    def first_at_least(limit):
        def halve(_, ends):
            low, high = ends
            middle = (low + high) // 2
            below = key_scalar[0, jnp.minimum(middle, edges - 1)] < limit
            go = low < high
            return (
                jnp.where(go & below, middle + 1, low),
                jnp.where(go & jnp.logical_not(below), middle, high),
            )

        ends = (jnp.int32(0), jnp.int32(edges))
        return lax.fori_loop(0, edges.bit_length(), halve, ends)[0]

    first = first_at_least(part * mesh_rows * mesh_rows)
    last = first_at_least((part + 1) * mesh_rows * mesh_rows)
    origin = first // 128 * 128

    def receiver_at(index):
        key = key_scalar[0, jnp.clip(index, 0, edges - 1)]
        return key // mesh_rows - part * mesh_rows

    def split(start, count):
        keys = key_ref[:, pl.ds(pl.multiple_of(start, 128), count)]
        column = as_column(keys)
        place = column & (mesh_rows - 1)
        receiver = lax.div(column, mesh_rows) - part * mesh_rows
        line = lax.div(keys, mesh_rows) - part * mesh_rows
        line = jnp.where((keys < 0) | (line < 0) | (line >= mesh_rows), -mesh_rows, line)
        return place, receiver, line

    table = table_ref[...]
    bases = []
    narrow = jnp.bool_(True)
    for block in range(BLOCKS):
        start = origin + block * EDGES
        low = receiver_at(jnp.maximum(start, first))
        high = receiver_at(jnp.minimum(start + EDGES, last) - 1)
        empty = start >= last
        base = jnp.where(empty, 0, low // ALIGN * ALIGN)
        narrow = narrow & (empty | (high - base < SPAN))
        bases.append(pl.multiple_of(base, ALIGN))

    @pl.when(narrow)
    def _():
        for block in range(BLOCKS):
            base = bases[block]
            place, receiver, line = split(origin + block * EDGES, EDGES)
            from_table = one_hot(place == iota((EDGES, mesh_rows), 1))
            from_recv = one_hot(receiver - base == iota((EDGES, SPAN), 1))
            window = pl.ds(base, SPAN)
            message = silu(dot(from_table, table) + dot(from_recv, recv_ref[window, :]))
            selector = one_hot(line - base == iota((SPAN, EDGES), 0))
            acc_ref[window, :] += dot(selector, message.astype(BF16))

    def general(block, carry):
        place, receiver, line = split(origin + block * FEW, FEW)
        from_table = one_hot(place == iota((FEW, mesh_rows), 1))
        from_recv = one_hot(receiver == iota((FEW, mesh_rows), 1))
        message = silu(dot(from_table, table) + dot(from_recv, recv_ref[:mesh_rows, :]))
        selector = one_hot(line == iota((mesh_rows, FEW), 0))
        acc_ref[:mesh_rows, :] += dot(selector, message.astype(BF16))
        return carry

    done = jnp.where(narrow, BLOCKS * EDGES // FEW, 0)
    lax.fori_loop(done, (last - origin + FEW - 1) // FEW, general, 0)


def own_kernel(
    key_in_ref,
    low_ref,
    high_ref,
    weight_ref,
    acc_ref,
    recv_ref,
    own_ref,
    key_ref,
    table_ref,
    key_scalar,
    sem,
):
    mesh_rows, width = table_ref.shape
    half = mesh_rows // 2
    copy = fetch_keys(key_in_ref, key_ref, key_scalar, sem)
    acc_ref[...] = jnp.zeros_like(acc_ref)
    recv_ref[mesh_rows:, :] = jnp.zeros((SPAN, width), BF16)
    for start, mid_ref in ((0, low_ref), (half, high_ref)):
        here = slice(start, start + half)
        mid = mid_ref[...]
        table_ref[here, :] = dot(mid, part(weight_ref, 0)[...]).astype(BF16)
        recv_ref[here, :] = dot(mid, part(weight_ref, 1)[...]).astype(BF16)
        own_ref[here, :] = dot(mid, part(weight_ref, 2)[...])
    copy.wait()
    edge_sums(0, key_scalar, key_ref, table_ref, recv_ref, acc_ref)


def near_kernel(
    key_in_ref,
    right_ref,
    left_ref,
    weight_ref,
    recv_ref,
    acc_in_ref,
    acc_ref,
    key_ref,
    table_ref,
    key_scalar,
    sem,
):
    half = table_ref.shape[0] // 2
    copy = fetch_keys(key_in_ref, key_ref, key_scalar, sem)
    acc_ref[...] = acc_in_ref[...]
    table_ref[:half, :] = dot(right_ref[...], part(weight_ref, 0)[...]).astype(BF16)
    table_ref[half:, :] = dot(left_ref[...], part(weight_ref, 0)[...]).astype(BF16)
    copy.wait()
    edge_sums(1, key_scalar, key_ref, table_ref, recv_ref, acc_ref)


def far_kernel(
    key_in_ref,
    right_ref,
    left_ref,
    weight_ref,
    recv_ref,
    acc_in_ref,
    low_ref,
    high_ref,
    own_ref,
    out_ref,
    key_ref,
    table_ref,
    acc_ref,
    key_scalar,
    sem,
):
    mesh_rows = table_ref.shape[0]
    half = mesh_rows // 2
    copy = fetch_keys(key_in_ref, key_ref, key_scalar, sem)
    acc_ref[...] = acc_in_ref[...]
    table_ref[:half, :] = dot(right_ref[...], part(weight_ref, 0)[...]).astype(BF16)
    table_ref[half:, :] = dot(left_ref[...], part(weight_ref, 0)[...]).astype(BF16)
    copy.wait()
    edge_sums(2, key_scalar, key_ref, table_ref, recv_ref, acc_ref)
    out_agg = part(weight_ref, 3)[...]
    for start, mid_ref in ((0, low_ref), (half, high_ref)):
        here = slice(start, start + half)
        update = own_ref[here, :] + dot(acc_ref[here, :].astype(BF16), out_agg)
        values = mid_ref[...].astype(F32) + silu(update)
        mean = jnp.mean(values, axis=-1, keepdims=True)
        centered = values - mean
        variance = jnp.mean(centered * centered, axis=-1, keepdims=True)
        out_ref[here, :] = centered * lax.rsqrt(variance + 1e-05)


def body(
    grid_feat,
    mesh_nodes,
    g2m_sender,
    g2m_receiver,
    send_counts,
    edge_sender,
    edge_receiver,
    embed_in,
    embed_out,
    proj_grid,
    proj_mesh,
    node_self,
    node_agg,
    edge_send,
    edge_recv,
    out_self,
    out_agg,
):
    owners = lax.axis_size(("band", "face"))
    faces = lax.axis_size("face")
    slots = g2m_sender.shape[1]
    grid_rows, feats = grid_feat.shape
    edges = edge_sender.shape[1]
    mesh_rows, width = mesh_nodes.shape
    half = mesh_rows // 2
    there = pl.BlockSpec(memory_space=pltpu.HBM)
    dma = pltpu.SemaphoreType.DMA
    weight = pltpu.VMEM((width, width), BF16)
    rows = pltpu.VMEM((mesh_rows, width), BF16)
    rows_half = pltpu.VMEM((half, width), BF16)
    rows_wide = pltpu.VMEM((mesh_rows, width), F32)
    sums = pltpu.VMEM((mesh_rows + SPAN, width), F32)

    packed, keys = call(
        functools.partial(pack_kernel, mesh_rows),
        (jax.ShapeDtypeStruct((slots, WIDE), BF16), jax.ShapeDtypeStruct((1, edges), I32)),
        (grid_feat.T, g2m_sender, g2m_receiver, send_counts, edge_sender, edge_receiver),
        (),
        scratch=[
            pltpu.VMEM((feats, grid_rows), BF16),
            pltpu.VMEM((1, slots), I32),
            pltpu.VMEM((1, slots), I32),
            pltpu.VMEM((1, owners), I32),
            pltpu.VMEM((1, edges), I32),
            pltpu.VMEM((1, edges), I32),
            pltpu.VMEM((slots, WIDE), BF16),
            pltpu.VMEM((1, edges), I32),
            dma((5,)),
            dma((4,)),
            dma((slots // SLOTS,)),
            dma,
        ],
        out_specs=(there, there),
    )
    keys = lax.sort(keys.reshape(edges), is_stable=False).reshape(1, edges)
    arrived = lax.all_to_all(
        packed.reshape(owners, slots // owners, WIDE),
        ("band", "face"),
        split_axis=0,
        concat_axis=0,
        tiled=True,
    ).reshape(slots, WIDE)
    fold, proj, own, keys = call(
        weights_kernel,
        (weight, rows, rows_wide, pltpu.VMEM((1, edges), I32)),
        (embed_out, proj_grid, mesh_nodes, proj_mesh, node_self, keys),
        (),
        scratch=[weight] * 2 + [rows] + [weight] * 2 + [dma((6,))],
    )
    embed = jnp.pad(embed_in, ((0, WIDE - feats), (0, 0)))
    low, high, weights = call(
        functools.partial(gather_kernel, feats),
        (rows_half, rows_half, pltpu.VMEM((4 * width, width), BF16)),
        (mesh_nodes, node_agg, edge_send, edge_recv, out_self, out_agg),
        (arrived, embed, fold, proj, own),
        scratch=[pltpu.VMEM((slots, width), BF16), rows, weight, dma((6,))],
    )

    forward = [(i, (i + 1) % faces) for i in range(faces)]
    backward = [(target, source) for source, target in forward]
    near, far = (
        (lax.ppermute(part, "face", backward), lax.ppermute(part, "face", forward))
        for part in (low, high)
    )
    key_scratch = [pltpu.VMEM((1, edges + BLOCKS * EDGES), I32)]
    key_scalars = [pltpu.SMEM((1, edges), I32), dma]
    acc, recv, own = call(
        own_kernel,
        (sums, pltpu.VMEM((mesh_rows + SPAN, width), BF16), rows_wide),
        (),
        (keys, low, high, weights),
        scratch=key_scratch + [rows] + key_scalars,
    )
    acc = call(
        near_kernel,
        sums,
        (),
        (keys, *near, weights, recv, acc),
        scratch=key_scratch + [rows] + key_scalars,
    )
    return call(
        far_kernel,
        jax.ShapeDtypeStruct((mesh_rows, width), F32),
        (),
        (keys, *far, weights, recv, acc, low, high, own),
        scratch=key_scratch + [rows, sums] + key_scalars,
    )


def solution(mesh):
    split = P(("band", "face"), None)
    return jax.shard_map(
        body,
        mesh=mesh,
        in_specs=(split,) * 7 + (P(),) * 10,
        out_specs=split,
        check_vma=False,
    )
```

```python
import functools

import jax
import jax.numpy as jnp
from jax import lax
from jax.experimental import pallas as pl
from jax.experimental.pallas import tpu as pltpu
from jax.sharding import PartitionSpec as P

BF16 = jnp.bfloat16
F32 = jnp.float32
I32 = jnp.int32
WIDE = 256
SLOTS = 1024
ARRIVED = 1024
BLOCKS = 3
EDGES = 512
PARTS = 3
FEW = 256
SPAN = 256
ALIGN = 16
VMEM_BYTES = 40 * 1024 * 1024


def dot(a, b):
    return jnp.dot(a, b, preferred_element_type=F32)


def dot_rows(a, b):
    return lax.dot_general(a, b, (((1,), (1,)), ((), ())), preferred_element_type=F32)


def silu(v):
    half = 0.5 * v
    return half + half * jnp.tanh(half)


def one_hot(hit):
    return jnp.where(hit, 1.0, 0.0).astype(BF16)


def iota(shape, dim):
    return lax.broadcasted_iota(I32, shape, dim)


def as_column(row):
    return jnp.broadcast_to(row, (8, row.shape[1])).T[:, 0:1]


def part(ref, index):
    rows = ref.shape[1]
    return ref.at[index * rows : (index + 1) * rows, :]


def start_copies(pairs, sems):
    copies = [
        pltpu.make_async_copy(source, target, sems.at[i]) for i, (source, target) in enumerate(pairs)
    ]
    for copy in copies:
        copy.start()
    return copies


def call(kernel, outs, hbm, vmem, scratch=(), out_specs=None, smem=(), aliases=None):
    def spec(space):
        return pl.BlockSpec(memory_space=space)

    if out_specs is None:
        out_specs = jax.tree.map(lambda _: spec(pltpu.VMEM), outs)
    args = list(smem)
    args += [pltpu.with_memory_space_constraint(arg, pltpu.HBM) for arg in hbm]
    args += [pltpu.with_memory_space_constraint(arg, pltpu.VMEM) for arg in vmem]
    spaces = [pltpu.SMEM] * len(smem) + [pltpu.HBM] * len(hbm) + [pltpu.VMEM] * len(vmem)
    return pl.pallas_call(
        kernel,
        out_shape=outs,
        in_specs=[spec(space) for space in spaces],
        out_specs=out_specs,
        scratch_shapes=list(scratch),
        input_output_aliases=aliases or {},
        compiler_params=pltpu.CompilerParams(vmem_limit_bytes=VMEM_BYTES),
    )(*args)


def pack_kernel(
    mesh_rows,
    feat_hbm,
    sender_hbm,
    receiver_hbm,
    count_hbm,
    from_hbm,
    to_hbm,
    out_hbm,
    key_hbm,
    feat_ref,
    sender_ref,
    receiver_ref,
    count_ref,
    from_ref,
    to_ref,
    column_ref,
    pad_ref,
    out_ref,
    key_ref,
    in_sem,
    feat_sem,
    out_sem,
    key_sem,
):
    feats, rows = feat_ref.shape
    slots = sender_ref.shape[1]
    owners = count_ref.shape[1]
    cap = slots // owners
    half = mesh_rows // 2
    small = start_copies(
        (
            (sender_hbm, sender_ref),
            (receiver_hbm, receiver_ref),
            (count_hbm, count_ref),
            (from_hbm, from_ref),
            (to_hbm, to_ref),
        ),
        in_sem,
    )
    pieces = feat_sem.shape[0]
    piece = rows // pieces
    cuts = [slice(i * piece, (i + 1) * piece) for i in range(pieces)]
    large = start_copies([(feat_hbm.at[:, cut], feat_ref.at[:, cut]) for cut in cuts], feat_sem)
    for copy in small:
        copy.wait()
    source = from_ref[...]
    row = lax.rem(source, mesh_rows)
    second = row // half
    mine = (source >= mesh_rows) & (source < 2 * mesh_rows)
    side = jnp.where(source < mesh_rows, half, 0)
    part = jnp.where(mine, 0, 1 + second)
    place = jnp.where(mine, row, row - second * half + side)
    key_ref[...] = (part * mesh_rows + to_ref[...]) * mesh_rows + place
    key_copy = pltpu.make_async_copy(key_ref, key_hbm, key_sem)
    key_copy.start()
    counts = jnp.broadcast_to(count_ref[...].astype(F32).astype(BF16), (8, owners))
    slot = iota((owners, slots), 1)
    first = iota((owners, slots), 0) * cap
    count = dot(counts, one_hot((slot >= first) & (slot < first + cap))).astype(I32)
    live = lax.rem(iota((8, slots), 1), cap) < count
    receiver = jnp.broadcast_to(receiver_ref[...], (8, slots))
    sender = jnp.broadcast_to(sender_ref[...], (8, slots))
    high = jnp.where(live, receiver >> 5, -1)
    low = jnp.where(live, receiver & 31, 0)
    line = iota((8, slots), 0)
    column_ref[...] = jnp.where(line == 0, sender, jnp.where(line == 1, high, low)).T
    for copy in large:
        copy.wait()
    whole = feats // ALIGN * ALIGN
    pad_ref[:whole, :] = feat_ref[:whole, :]
    line = iota((WIDE - whole, rows), 0)
    rest = jnp.zeros((WIDE - whole, rows), F32)
    for i in range(whole, feats):
        rest = jnp.where(line == i - whole, feat_ref[i : i + 1, :].astype(F32), rest)
    pad_ref[whole:, :] = rest.astype(BF16)

    def leave(block):
        here = pl.ds(pl.multiple_of(block * SLOTS, SLOTS), SLOTS)
        return pltpu.make_async_copy(out_ref.at[here, :], out_hbm.at[here, :], out_sem.at[block])

    def step(block, carry):
        start = pl.multiple_of(block * SLOTS, SLOTS)
        here = pl.ds(start, SLOTS)
        columns = column_ref[here, :]
        picker = one_hot(columns[:, 0:1] == iota((SLOTS, rows), 1))
        column = iota((SLOTS, WIDE), 1)
        digits = jnp.where(
            column == feats, columns[:, 1:2], jnp.where(column == feats + 1, columns[:, 2:3], 0)
        )
        out_ref[here, :] = (dot_rows(picker, pad_ref[...]) + digits.astype(F32)).astype(BF16)
        leave(block).start()
        return carry

    lax.fori_loop(0, slots // SLOTS, step, 0)
    for block in range(slots // SLOTS):
        leave(block).wait()
    key_copy.wait()


def weights_kernel(
    embed_out_hbm,
    proj_grid_hbm,
    mesh_hbm,
    proj_mesh_hbm,
    node_self_hbm,
    key_hbm,
    fold_ref,
    proj_ref,
    self_ref,
    key_ref,
    plan_ref,
    embed_out_ref,
    proj_grid_ref,
    mesh_ref,
    proj_mesh_ref,
    node_self_ref,
    key_scalar,
    sems,
):
    edges = key_hbm.shape[1]
    pairs = (
        (embed_out_hbm, embed_out_ref),
        (proj_grid_hbm, proj_grid_ref),
        (mesh_hbm, mesh_ref),
        (proj_mesh_hbm, proj_mesh_ref),
        (node_self_hbm, node_self_ref),
        (key_hbm, key_ref.at[:, :edges]),
        (key_hbm, key_scalar),
    )
    copies = start_copies(pairs, sems)
    key_ref[:, edges:] = jnp.full((1, key_ref.shape[1] - edges), -1, I32)
    for copy in copies:
        copy.wait()
    plan_edges(key_scalar, plan_ref, mesh_ref.shape[0])
    fold_ref[...] = dot(embed_out_ref[...], proj_grid_ref[...]).astype(BF16)
    mesh = mesh_ref[...]
    proj_ref[...] = dot(mesh, proj_mesh_ref[...]).astype(BF16)
    self_ref[...] = dot(mesh, node_self_ref[...])


def gather_kernel(
    feats,
    mesh_hbm,
    node_agg_hbm,
    edge_send_hbm,
    edge_recv_hbm,
    out_self_hbm,
    out_agg_hbm,
    x_ref,
    embed_ref,
    fold_ref,
    proj_ref,
    self_ref,
    low_ref,
    high_ref,
    weight_ref,
    sum_ref,
    mesh_ref,
    node_agg_ref,
    sems,
):
    pairs = (
        (mesh_hbm, mesh_ref),
        (node_agg_hbm, node_agg_ref),
        (edge_send_hbm, part(weight_ref, 0)),
        (edge_recv_hbm, part(weight_ref, 1)),
        (out_self_hbm, part(weight_ref, 2)),
        (out_agg_hbm, part(weight_ref, 3)),
    )
    copies = start_copies(pairs, sems)
    slots = x_ref.shape[0]
    mesh_rows = mesh_ref.shape[0]
    half = mesh_rows // 2

    def weight(place):
        return jnp.where(place == feats, 32.0, jnp.where(place == feats + 1, 1.0, 0.0)).astype(BF16)

    across = weight(iota((WIDE, 128), 0))
    along = weight(iota((8, WIDE), 1))
    sum_ref[...] = jnp.zeros_like(sum_ref)

    def step(block, carry):
        x = x_ref[pl.ds(pl.multiple_of(block * ARRIVED, ARRIVED), ARRIVED), :]
        hidden = silu(dot(x, embed_ref[...])).astype(BF16)
        column = dot(x, across).astype(I32)[:, 0:1]
        picker = one_hot(column == iota((ARRIVED, mesh_rows), 1))
        message = silu(dot(hidden, fold_ref[...]) + dot(picker, proj_ref[...])).astype(BF16)
        line = dot_rows(along, x).astype(I32)[0:1, :]
        selector = one_hot(line == iota((mesh_rows, ARRIVED), 0))
        sum_ref[...] += dot(selector, message)
        return carry

    lax.fori_loop(0, slots // ARRIVED, step, 0)
    for copy in copies:
        copy.wait()
    for start, out_ref in ((0, low_ref), (half, high_ref)):
        here = slice(start, start + half)
        inner = self_ref[here, :] + dot(sum_ref[here, :].astype(BF16), node_agg_ref[...])
        out_ref[...] = (mesh_ref[here, :].astype(F32) + silu(inner)).astype(BF16)


def plan_edges(key_scalar, plan_ref, mesh_rows):
    edges = key_scalar.shape[1]

    def first_at_least(limit):
        def halve(_, ends):
            low, high = ends
            middle = (low + high) // 2
            below = key_scalar[0, jnp.minimum(middle, edges - 1)] < limit
            go = low < high
            return (
                jnp.where(go & below, middle + 1, low),
                jnp.where(go & jnp.logical_not(below), middle, high),
            )

        ends = (jnp.int32(0), jnp.int32(edges))
        return lax.fori_loop(0, edges.bit_length(), halve, ends)[0]

    first = jnp.int32(0)
    for index in range(PARTS):
        last = jnp.int32(edges)
        if index < PARTS - 1:
            last = first_at_least((index + 1) * mesh_rows * mesh_rows)
        origin = first // 128 * 128

        def receiver_at(place):
            key = key_scalar[0, jnp.clip(place, 0, edges - 1)]
            return key // mesh_rows - index * mesh_rows

        narrow = jnp.bool_(True)
        for block in range(BLOCKS):
            start = origin + block * EDGES
            low = receiver_at(jnp.maximum(start, first))
            high = receiver_at(jnp.minimum(start + EDGES, last) - 1)
            empty = start >= last
            base = jnp.where(empty, 0, low // ALIGN * ALIGN)
            narrow = narrow & (empty | (high - base < SPAN))
            plan_ref[index, 3 + block] = base
        plan_ref[index, 0] = origin
        plan_ref[index, 1] = last
        plan_ref[index, 2] = narrow.astype(I32)
        first = last


def edge_sums(index, plan_ref, key_ref, table_ref, recv_ref, acc_ref):
    mesh_rows = table_ref.shape[0]
    origin = plan_ref[index, 0]
    last = plan_ref[index, 1]
    narrow = plan_ref[index, 2] == 1

    def split(start, count):
        keys = key_ref[:, pl.ds(pl.multiple_of(start, 128), count)]
        column = as_column(keys)
        place = column & (mesh_rows - 1)
        receiver = lax.div(column, mesh_rows) - index * mesh_rows
        line = lax.div(keys, mesh_rows) - index * mesh_rows
        line = jnp.where((keys < 0) | (line < 0) | (line >= mesh_rows), -mesh_rows, line)
        return place, receiver, line

    @pl.when(narrow)
    def _():
        for block in range(BLOCKS):
            base = pl.multiple_of(plan_ref[index, 3 + block], ALIGN)
            place, receiver, line = split(origin + block * EDGES, EDGES)
            from_table = one_hot(place == iota((EDGES, mesh_rows), 1))
            from_recv = one_hot(receiver - base == iota((EDGES, SPAN), 1))
            reach = pl.ds(base, SPAN)
            message = silu(dot(from_table, table_ref[...]) + dot(from_recv, recv_ref[reach, :]))
            selector = one_hot(line - base == iota((SPAN, EDGES), 0))
            acc_ref[reach, :] += dot(selector, message.astype(BF16))
    def general(block, carry):
        place, receiver, line = split(origin + block * FEW, FEW)
        from_table = one_hot(place == iota((FEW, mesh_rows), 1))
        from_recv = one_hot(receiver == iota((FEW, mesh_rows), 1))
        message = silu(dot(from_table, table_ref[...]) + dot(from_recv, recv_ref[:mesh_rows, :]))
        selector = one_hot(line == iota((mesh_rows, FEW), 0))
        acc_ref[:mesh_rows, :] += dot(selector, message.astype(BF16))
        return carry

    done = jnp.where(narrow, BLOCKS * EDGES // FEW, 0)
    lax.fori_loop(done, (last - origin + FEW - 1) // FEW, general, 0)


def own_kernel(
    plan_ref, key_ref, low_ref, high_ref, weight_ref, acc_ref, recv_ref, own_ref, later_ref, table_ref
):
    mesh_rows, width = table_ref.shape
    half = mesh_rows // 2
    acc_ref[...] = jnp.zeros_like(acc_ref)
    recv_ref[mesh_rows:, :] = jnp.zeros((SPAN, width), BF16)
    later_ref[...] = high_ref[...]
    for start, mid_ref in ((0, low_ref), (half, high_ref)):
        here = slice(start, start + half)
        mid = mid_ref[...]
        table_ref[here, :] = dot(mid, part(weight_ref, 0)[...]).astype(BF16)
        recv_ref[here, :] = dot(mid, part(weight_ref, 1)[...]).astype(BF16)
        own_ref[here, :] = dot(mid, part(weight_ref, 2)[...])
    edge_sums(0, plan_ref, key_ref, table_ref, recv_ref, acc_ref)


def near_kernel(
    plan_ref, acc_in_ref, key_ref, right_ref, left_ref, weight_ref, recv_ref, acc_ref, table_ref
):
    half = table_ref.shape[0] // 2
    table_ref[:half, :] = dot(right_ref[...], part(weight_ref, 0)[...]).astype(BF16)
    table_ref[half:, :] = dot(left_ref[...], part(weight_ref, 0)[...]).astype(BF16)
    edge_sums(1, plan_ref, key_ref, table_ref, recv_ref, acc_ref)


def far_kernel(
    plan_ref,
    acc_in_ref,
    key_ref,
    right_ref,
    left_ref,
    weight_ref,
    recv_ref,
    low_ref,
    high_ref,
    own_ref,
    out_hbm,
    table_ref,
    acc_ref,
    out_ref,
    sems,
):
    mesh_rows = table_ref.shape[0]
    half = mesh_rows // 2
    acc_ref[...] = acc_in_ref[...]
    table_ref[:half, :] = dot(right_ref[...], part(weight_ref, 0)[...]).astype(BF16)
    table_ref[half:, :] = dot(left_ref[...], part(weight_ref, 0)[...]).astype(BF16)
    edge_sums(2, plan_ref, key_ref, table_ref, recv_ref, acc_ref)
    copies = []
    rows = mesh_rows // sems.shape[0]
    for index in range(sems.shape[0]):
        start = index * rows
        here = slice(start, start + rows)
        update = own_ref[here, :] + dot(acc_ref[here, :].astype(BF16), part(weight_ref, 3)[...])
        mid_ref = low_ref if start < half else high_ref
        mid = mid_ref[start % half : start % half + rows, :]
        values = mid.astype(F32) + silu(update)
        mean = jnp.mean(values, axis=-1, keepdims=True)
        centered = values - mean
        variance = jnp.mean(centered * centered, axis=-1, keepdims=True)
        out_ref[here, :] = centered * lax.rsqrt(variance + 1e-05)
        copies += start_copies([(out_ref.at[here, :], out_hbm.at[here, :])], sems.at[index : index + 1])
    for copy in copies:
        copy.wait()


def body(
    grid_feat,
    mesh_nodes,
    g2m_sender,
    g2m_receiver,
    send_counts,
    edge_sender,
    edge_receiver,
    embed_in,
    embed_out,
    proj_grid,
    proj_mesh,
    node_self,
    node_agg,
    edge_send,
    edge_recv,
    out_self,
    out_agg,
):
    owners = lax.axis_size(("band", "face"))
    faces = lax.axis_size("face")
    slots = g2m_sender.shape[1]
    grid_rows, feats = grid_feat.shape
    edges = edge_sender.shape[1]
    mesh_rows, width = mesh_nodes.shape
    half = mesh_rows // 2
    there = pl.BlockSpec(memory_space=pltpu.HBM)
    dma = pltpu.SemaphoreType.DMA
    weight = pltpu.VMEM((width, width), BF16)
    rows = pltpu.VMEM((mesh_rows, width), BF16)
    rows_half = pltpu.VMEM((half, width), BF16)
    rows_wide = pltpu.VMEM((mesh_rows, width), F32)
    sums = pltpu.VMEM((mesh_rows + SPAN, width), F32)

    packed, keys = call(
        functools.partial(pack_kernel, mesh_rows),
        (jax.ShapeDtypeStruct((slots, WIDE), BF16), jax.ShapeDtypeStruct((1, edges), I32)),
        (grid_feat.T, g2m_sender, g2m_receiver, send_counts, edge_sender, edge_receiver),
        (),
        scratch=[
            pltpu.VMEM((feats, grid_rows), BF16),
            pltpu.VMEM((1, slots), I32),
            pltpu.VMEM((1, slots), I32),
            pltpu.VMEM((1, owners), I32),
            pltpu.VMEM((1, edges), I32),
            pltpu.VMEM((1, edges), I32),
            pltpu.VMEM((slots, 8), I32),
            pltpu.VMEM((WIDE, grid_rows), BF16),
            pltpu.VMEM((slots, WIDE), BF16),
            pltpu.VMEM((1, edges), I32),
            dma((5,)),
            dma((4,)),
            dma((slots // SLOTS,)),
            dma,
        ],
        out_specs=(there, there),
    )
    keys = lax.sort(keys.reshape(edges), is_stable=False).reshape(1, edges)
    arrived = lax.all_to_all(
        packed.reshape(owners, slots // owners, WIDE),
        ("band", "face"),
        split_axis=0,
        concat_axis=0,
        tiled=True,
    ).reshape(slots, WIDE)
    fold, proj, own, keys, plan = call(
        weights_kernel,
        (
            weight,
            rows,
            rows_wide,
            pltpu.VMEM((1, edges + BLOCKS * EDGES), I32),
            jax.ShapeDtypeStruct((PARTS, 3 + BLOCKS), I32),
        ),
        (embed_out, proj_grid, mesh_nodes, proj_mesh, node_self, keys),
        (),
        scratch=[weight] * 2 + [rows] + [weight] * 2 + [pltpu.SMEM((1, edges), I32), dma((7,))],
        out_specs=[pl.BlockSpec(memory_space=pltpu.VMEM)] * 4 + [pl.BlockSpec(memory_space=pltpu.SMEM)],
    )
    embed = jnp.pad(embed_in, ((0, WIDE - feats), (0, 0)))
    low, high, weights = call(
        functools.partial(gather_kernel, feats),
        (rows_half, rows_half, pltpu.VMEM((4 * width, width), BF16)),
        (mesh_nodes, node_agg, edge_send, edge_recv, out_self, out_agg),
        (arrived, embed, fold, proj, own),
        scratch=[rows_wide, rows, weight, dma((6,))],
    )

    forward = [(i, (i + 1) % faces) for i in range(faces)]
    backward = [(target, source) for source, target in forward]

    def neighbours(rows):
        return lax.ppermute(rows, "face", backward), lax.ppermute(rows, "face", forward)

    near = neighbours(low)
    acc, recv, own, later = call(
        own_kernel,
        (sums, pltpu.VMEM((mesh_rows + SPAN, width), BF16), rows_wide, rows_half),
        (),
        (keys, low, high, weights),
        scratch=[rows],
        smem=(plan,),
    )
    far = neighbours(later)
    acc = call(
        near_kernel,
        sums,
        (),
        (acc, keys, *near, weights, recv),
        scratch=[rows],
        smem=(plan,),
        aliases={1: 0},
    )
    return call(
        far_kernel,
        jax.ShapeDtypeStruct((mesh_rows, width), F32),
        (),
        (acc, keys, *far, weights, recv, low, high, own),
        scratch=[rows, sums, rows_wide, dma((4,))],
        out_specs=there,
        smem=(plan,),
    )


def solution(mesh):
    split = P(("band", "face"), None)
    return jax.shard_map(
        body,
        mesh=mesh,
        in_specs=(split,) * 7 + (P(),) * 10,
        out_specs=split,
        check_vma=False,
    )
```

```python
import functools

import jax
import jax.numpy as jnp
from jax import lax
from jax.experimental import pallas as pl
from jax.experimental.pallas import tpu as pltpu
from jax.sharding import PartitionSpec as P

BF16 = jnp.bfloat16
F32 = jnp.float32
I32 = jnp.int32
WIDE = 256
DEAD = 1024
SLOTS = 1024
ARRIVED = 1024
BLOCKS = 3
EDGES = 512
PARTS = 3
FEW = 256
SPAN = 256
ALIGN = 16
VMEM_BYTES = 40 * 1024 * 1024


def dot(a, b):
    return jnp.dot(a, b, preferred_element_type=F32)


def dot_rows(a, b):
    return lax.dot_general(a, b, (((1,), (1,)), ((), ())), preferred_element_type=F32)


def silu(v):
    half = 0.5 * v
    return half + half * jnp.tanh(half)


def one_hot(hit):
    return jnp.where(hit, 1.0, 0.0).astype(BF16)


def iota(shape, dim):
    return lax.broadcasted_iota(I32, shape, dim)


def receiver_code(receiver):
    return jnp.where(receiver <= DEAD // 4, receiver, DEAD // 4 - receiver)


def as_column(row):
    return jnp.broadcast_to(row, (8, row.shape[1])).T[:, 0:1]


def part(ref, index):
    rows = ref.shape[1]
    return ref.at[index * rows : (index + 1) * rows, :]


def start_copies(pairs, sems):
    copies = [
        pltpu.make_async_copy(source, target, sems.at[i]) for i, (source, target) in enumerate(pairs)
    ]
    for copy in copies:
        copy.start()
    return copies


def call(kernel, outs, hbm, vmem, scratch=(), out_specs=None, smem=(), aliases=None):
    def spec(space):
        return pl.BlockSpec(memory_space=space)

    if out_specs is None:
        out_specs = jax.tree.map(lambda _: spec(pltpu.VMEM), outs)
    args = list(smem)
    args += [pltpu.with_memory_space_constraint(arg, pltpu.HBM) for arg in hbm]
    args += [pltpu.with_memory_space_constraint(arg, pltpu.VMEM) for arg in vmem]
    spaces = [pltpu.SMEM] * len(smem) + [pltpu.HBM] * len(hbm) + [pltpu.VMEM] * len(vmem)
    return pl.pallas_call(
        kernel,
        out_shape=outs,
        in_specs=[spec(space) for space in spaces],
        out_specs=out_specs,
        scratch_shapes=list(scratch),
        input_output_aliases=aliases or {},
        compiler_params=pltpu.CompilerParams(vmem_limit_bytes=VMEM_BYTES),
    )(*args)


def pack_kernel(
    mesh_rows,
    feat_hbm,
    sender_hbm,
    receiver_hbm,
    count_hbm,
    from_hbm,
    to_hbm,
    out_hbm,
    key_hbm,
    feat_ref,
    sender_ref,
    receiver_ref,
    count_ref,
    from_ref,
    to_ref,
    column_ref,
    pad_ref,
    out_ref,
    key_ref,
    in_sem,
    feat_sem,
    out_sem,
    key_sem,
):
    feats, rows = feat_ref.shape
    slots = sender_ref.shape[1]
    owners = count_ref.shape[1]
    cap = slots // owners
    half = mesh_rows // 2
    small = start_copies(
        (
            (sender_hbm, sender_ref),
            (receiver_hbm, receiver_ref),
            (count_hbm, count_ref),
            (from_hbm, from_ref),
            (to_hbm, to_ref),
        ),
        in_sem,
    )
    pieces = feat_sem.shape[0]
    piece = rows // pieces
    cuts = [slice(i * piece, (i + 1) * piece) for i in range(pieces)]
    large = start_copies([(feat_hbm.at[:, cut], feat_ref.at[:, cut]) for cut in cuts], feat_sem)
    for copy in small:
        copy.wait()
    source = from_ref[...]
    row = lax.rem(source, mesh_rows)
    second = row // half
    mine = (source >= mesh_rows) & (source < 2 * mesh_rows)
    side = jnp.where(source < mesh_rows, half, 0)
    part = jnp.where(mine, 0, 1 + second)
    place = jnp.where(mine, row, row - second * half + side)
    key_ref[...] = (part * mesh_rows + to_ref[...]) * mesh_rows + place
    key_copy = pltpu.make_async_copy(key_ref, key_hbm, key_sem)
    key_copy.start()
    counts = jnp.broadcast_to(count_ref[...].astype(F32).astype(BF16), (8, owners))
    slot = iota((owners, slots), 1)
    first = iota((owners, slots), 0) * cap
    count = dot(counts, one_hot((slot >= first) & (slot < first + cap))).astype(I32)
    live = lax.rem(iota((8, slots), 1), cap) < count
    receiver = jnp.broadcast_to(receiver_ref[...], (8, slots))
    sender = jnp.broadcast_to(sender_ref[...], (8, slots))
    code = jnp.where(live, receiver_code(receiver), DEAD)
    column_ref[...] = jnp.where(iota((8, slots), 0) == 0, sender, code).T
    for copy in large:
        copy.wait()
    whole = feats // ALIGN * ALIGN
    pad_ref[:whole, :] = feat_ref[:whole, :]
    line = iota((WIDE - whole, rows), 0)
    rest = jnp.zeros((WIDE - whole, rows), F32)
    for i in range(whole, feats):
        rest = jnp.where(line == i - whole, feat_ref[i : i + 1, :].astype(F32), rest)
    pad_ref[whole:, :] = rest.astype(BF16)

    def leave(block):
        here = pl.ds(pl.multiple_of(block * SLOTS, SLOTS), SLOTS)
        return pltpu.make_async_copy(out_ref.at[here, :], out_hbm.at[here, :], out_sem.at[block])

    def step(block, carry):
        start = pl.multiple_of(block * SLOTS, SLOTS)
        here = pl.ds(start, SLOTS)
        columns = column_ref[here, :]
        picker = one_hot(columns[:, 0:1] == iota((SLOTS, rows), 1))
        column = iota((SLOTS, WIDE), 1)
        code = jnp.where(column == feats, columns[:, 1:2], 0).astype(F32)
        out_ref[here, :] = (dot_rows(picker, pad_ref[...]) + code).astype(BF16)
        leave(block).start()
        return carry

    lax.fori_loop(0, slots // SLOTS, step, 0)
    for block in range(slots // SLOTS):
        leave(block).wait()
    key_copy.wait()


def weights_kernel(
    embed_out_hbm,
    proj_grid_hbm,
    mesh_hbm,
    proj_mesh_hbm,
    node_self_hbm,
    key_hbm,
    fold_ref,
    proj_ref,
    self_ref,
    key_ref,
    plan_ref,
    embed_out_ref,
    proj_grid_ref,
    mesh_ref,
    proj_mesh_ref,
    node_self_ref,
    key_scalar,
    sems,
):
    edges = key_hbm.shape[1]
    pairs = (
        (embed_out_hbm, embed_out_ref),
        (proj_grid_hbm, proj_grid_ref),
        (mesh_hbm, mesh_ref),
        (proj_mesh_hbm, proj_mesh_ref),
        (node_self_hbm, node_self_ref),
        (key_hbm, key_ref.at[:, :edges]),
        (key_hbm, key_scalar),
    )
    copies = start_copies(pairs, sems)
    key_ref[:, edges:] = jnp.full((1, key_ref.shape[1] - edges), -1, I32)
    for copy in copies:
        copy.wait()
    plan_edges(key_scalar, plan_ref, mesh_ref.shape[0])
    fold_ref[...] = dot(embed_out_ref[...], proj_grid_ref[...]).astype(BF16)
    mesh = mesh_ref[...]
    proj_ref[...] = dot(mesh, proj_mesh_ref[...]).astype(BF16)
    self_ref[...] = dot(mesh, node_self_ref[...])


def next_rows(sums, own, mesh, node_agg):
    inner = own + dot(sums.astype(BF16), node_agg)
    return (mesh.astype(F32) + silu(inner)).astype(BF16)


def gather_kernel(
    feats,
    mesh_hbm,
    node_agg_hbm,
    edge_send_hbm,
    edge_recv_hbm,
    out_self_hbm,
    out_agg_hbm,
    x_ref,
    embed_ref,
    fold_ref,
    proj_ref,
    self_ref,
    low_ref,
    send_ref,
    msg_ref,
    line_ref,
    weight_ref,
    sum_ref,
    sems,
):
    sources = (edge_send_hbm, edge_recv_hbm, out_self_hbm, out_agg_hbm, node_agg_hbm, mesh_hbm)
    copies = start_copies([(hbm, part(weight_ref, i)) for i, hbm in enumerate(sources)], sems)
    slots = x_ref.shape[0]
    mesh_rows = self_ref.shape[0]
    half = mesh_rows // 2
    lanes = feats // 128 * 128
    along = one_hot(iota((8, WIDE - lanes), 1) == feats - lanes)
    sum_ref[...] = jnp.zeros_like(sum_ref)

    def step(block, carry):
        here = pl.ds(pl.multiple_of(block * ARRIVED, ARRIVED), ARRIVED)
        x = x_ref[here, :]
        hidden = silu(dot(x, embed_ref[...])).astype(BF16)
        column = x[:, feats : feats + 1].astype(F32)
        codes = receiver_code(iota((ARRIVED, mesh_rows), 1)).astype(F32)
        picker = one_hot(column == codes)
        message = silu(dot(hidden, fold_ref[...]) + dot(picker, proj_ref[...])).astype(BF16)
        msg_ref[here, :] = message
        line = dot_rows(along, x[:, lanes:])
        line_ref[:, here] = line
        codes = receiver_code(iota((half, ARRIVED), 0)).astype(F32)
        sum_ref[...] += dot(one_hot(line[0:1, :] == codes), message)
        return carry

    lax.fori_loop(0, slots // ARRIVED, step, 0)
    for copy in copies:
        copy.wait()
    mesh = part(weight_ref, 5)[:half, :]
    low_ref[...] = next_rows(sum_ref[...], self_ref[:half, :], mesh, part(weight_ref, 4)[...])
    send_ref[...] = dot(low_ref[...], part(weight_ref, 0)[...]).astype(BF16)


def plan_edges(key_scalar, plan_ref, mesh_rows):
    edges = key_scalar.shape[1]

    def first_at_least(limit):
        def halve(_, ends):
            low, high = ends
            middle = (low + high) // 2
            below = key_scalar[0, jnp.minimum(middle, edges - 1)] < limit
            go = low < high
            return (
                jnp.where(go & below, middle + 1, low),
                jnp.where(go & jnp.logical_not(below), middle, high),
            )

        ends = (jnp.int32(0), jnp.int32(edges))
        return lax.fori_loop(0, edges.bit_length(), halve, ends)[0]

    first = jnp.int32(0)
    for index in range(PARTS):
        last = jnp.int32(edges)
        if index < PARTS - 1:
            last = first_at_least((index + 1) * mesh_rows * mesh_rows)
        origin = first // 128 * 128

        def receiver_at(place):
            key = key_scalar[0, jnp.clip(place, 0, edges - 1)]
            return key // mesh_rows - index * mesh_rows

        narrow = jnp.bool_(True)
        for block in range(BLOCKS):
            start = origin + block * EDGES
            low = receiver_at(jnp.maximum(start, first))
            high = receiver_at(jnp.minimum(start + EDGES, last) - 1)
            empty = start >= last
            base = jnp.where(empty, 0, low // ALIGN * ALIGN)
            narrow = narrow & (empty | (high - base < SPAN))
            plan_ref[index, 3 + block] = base
        plan_ref[index, 0] = origin
        plan_ref[index, 1] = last
        plan_ref[index, 2] = narrow.astype(I32)
        first = last


def edge_sums(index, plan_ref, key_ref, table_ref, recv_ref, acc_ref):
    mesh_rows = table_ref.shape[0]
    origin = plan_ref[index, 0]
    last = plan_ref[index, 1]
    narrow = plan_ref[index, 2] == 1

    def split(start, count):
        keys = key_ref[:, pl.ds(pl.multiple_of(start, 128), count)]
        column = as_column(keys)
        place = column & (mesh_rows - 1)
        receiver = lax.div(column, mesh_rows) - index * mesh_rows
        line = lax.div(keys, mesh_rows) - index * mesh_rows
        line = jnp.where((keys < 0) | (line < 0) | (line >= mesh_rows), -mesh_rows, line)
        return place, receiver, line

    @pl.when(narrow)
    def _():
        for block in range(BLOCKS):
            base = pl.multiple_of(plan_ref[index, 3 + block], ALIGN)
            place, receiver, line = split(origin + block * EDGES, EDGES)
            from_table = one_hot(place == iota((EDGES, mesh_rows), 1))
            from_recv = one_hot(receiver - base == iota((EDGES, SPAN), 1))
            reach = pl.ds(base, SPAN)
            message = silu(dot(from_table, table_ref[...]) + dot(from_recv, recv_ref[reach, :]))
            selector = one_hot(line - base == iota((SPAN, EDGES), 0))
            acc_ref[reach, :] += dot(selector, message.astype(BF16))
    def general(block, carry):
        place, receiver, line = split(origin + block * FEW, FEW)
        from_table = one_hot(place == iota((FEW, mesh_rows), 1))
        from_recv = one_hot(receiver == iota((FEW, mesh_rows), 1))
        message = silu(dot(from_table, table_ref[...]) + dot(from_recv, recv_ref[:mesh_rows, :]))
        selector = one_hot(line == iota((mesh_rows, FEW), 0))
        acc_ref[:mesh_rows, :] += dot(selector, message.astype(BF16))
        return carry

    done = jnp.where(narrow, BLOCKS * EDGES // FEW, 0)
    lax.fori_loop(done, (last - origin + FEW - 1) // FEW, general, 0)


def own_kernel(
    plan_ref,
    key_ref,
    low_ref,
    send_low_ref,
    msg_ref,
    line_ref,
    self_ref,
    weight_ref,
    acc_ref,
    recv_ref,
    own_ref,
    high_ref,
    send_high_ref,
    table_ref,
):
    mesh_rows, width = table_ref.shape
    half = mesh_rows // 2
    codes = receiver_code(iota((half, msg_ref.shape[0]), 0) + half).astype(F32)
    sums = dot(one_hot(line_ref[0:1, :] == codes), msg_ref[...])
    mesh = part(weight_ref, 5)[half:, :]
    high_ref[...] = next_rows(sums, self_ref[half:, :], mesh, part(weight_ref, 4)[...])
    send_high_ref[...] = dot(high_ref[...], part(weight_ref, 0)[...]).astype(BF16)
    table_ref[:half, :] = send_low_ref[...]
    table_ref[half:, :] = send_high_ref[...]
    acc_ref[...] = jnp.zeros_like(acc_ref)
    recv_ref[mesh_rows:, :] = jnp.zeros((SPAN, width), BF16)
    for start, mid_ref in ((0, low_ref), (half, high_ref)):
        here = slice(start, start + half)
        mid = mid_ref[...]
        recv_ref[here, :] = dot(mid, part(weight_ref, 1)[...]).astype(BF16)
        own_ref[here, :] = dot(mid, part(weight_ref, 2)[...])
    edge_sums(0, plan_ref, key_ref, table_ref, recv_ref, acc_ref)


def near_kernel(plan_ref, acc_in_ref, key_ref, right_ref, left_ref, recv_ref, acc_ref, table_ref):
    half = table_ref.shape[0] // 2
    table_ref[:half, :] = right_ref[...]
    table_ref[half:, :] = left_ref[...]
    edge_sums(1, plan_ref, key_ref, table_ref, recv_ref, acc_ref)


def far_kernel(
    plan_ref,
    acc_in_ref,
    key_ref,
    right_ref,
    left_ref,
    weight_ref,
    recv_ref,
    low_ref,
    high_ref,
    own_ref,
    out_hbm,
    acc_ref,
    table_ref,
    out_ref,
    sems,
):
    mesh_rows = table_ref.shape[0]
    half = mesh_rows // 2
    table_ref[:half, :] = right_ref[...]
    table_ref[half:, :] = left_ref[...]
    edge_sums(2, plan_ref, key_ref, table_ref, recv_ref, acc_ref)
    copies = []
    rows = mesh_rows // sems.shape[0]
    for index in range(sems.shape[0]):
        start = index * rows
        here = slice(start, start + rows)
        update = own_ref[here, :] + dot(acc_ref[here, :].astype(BF16), part(weight_ref, 3)[...])
        mid_ref = low_ref if start < half else high_ref
        mid = mid_ref[start % half : start % half + rows, :]
        values = mid.astype(F32) + silu(update)
        mean = jnp.mean(values, axis=-1, keepdims=True)
        centered = values - mean
        variance = jnp.mean(centered * centered, axis=-1, keepdims=True)
        out_ref[here, :] = centered * lax.rsqrt(variance + 1e-05)
        copies += start_copies([(out_ref.at[here, :], out_hbm.at[here, :])], sems.at[index : index + 1])
    for copy in copies:
        copy.wait()


def body(
    grid_feat,
    mesh_nodes,
    g2m_sender,
    g2m_receiver,
    send_counts,
    edge_sender,
    edge_receiver,
    embed_in,
    embed_out,
    proj_grid,
    proj_mesh,
    node_self,
    node_agg,
    edge_send,
    edge_recv,
    out_self,
    out_agg,
):
    owners = lax.axis_size(("band", "face"))
    faces = lax.axis_size("face")
    slots = g2m_sender.shape[1]
    grid_rows, feats = grid_feat.shape
    edges = edge_sender.shape[1]
    mesh_rows, width = mesh_nodes.shape
    half = mesh_rows // 2
    there = pl.BlockSpec(memory_space=pltpu.HBM)
    dma = pltpu.SemaphoreType.DMA
    weight = pltpu.VMEM((width, width), BF16)
    rows = pltpu.VMEM((mesh_rows, width), BF16)
    rows_half = pltpu.VMEM((half, width), BF16)
    rows_wide = pltpu.VMEM((mesh_rows, width), F32)
    sums = pltpu.VMEM((mesh_rows + SPAN, width), F32)

    packed, keys = call(
        functools.partial(pack_kernel, mesh_rows),
        (jax.ShapeDtypeStruct((slots, WIDE), BF16), jax.ShapeDtypeStruct((1, edges), I32)),
        (grid_feat.T, g2m_sender, g2m_receiver, send_counts, edge_sender, edge_receiver),
        (),
        scratch=[
            pltpu.VMEM((feats, grid_rows), BF16),
            pltpu.VMEM((1, slots), I32),
            pltpu.VMEM((1, slots), I32),
            pltpu.VMEM((1, owners), I32),
            pltpu.VMEM((1, edges), I32),
            pltpu.VMEM((1, edges), I32),
            pltpu.VMEM((slots, 8), I32),
            pltpu.VMEM((WIDE, grid_rows), BF16),
            pltpu.VMEM((slots, WIDE), BF16),
            pltpu.VMEM((1, edges), I32),
            dma((5,)),
            dma((1,)),
            dma((slots // SLOTS,)),
            dma,
        ],
        out_specs=(there, there),
    )
    keys = lax.sort(keys.reshape(edges), is_stable=False).reshape(1, edges)
    arrived = lax.all_to_all(
        packed.reshape(owners, slots // owners, WIDE),
        ("band", "face"),
        split_axis=0,
        concat_axis=0,
        tiled=True,
    ).reshape(slots, WIDE)
    fold, proj, own, keys, plan = call(
        weights_kernel,
        (
            weight,
            rows,
            rows_wide,
            pltpu.VMEM((1, edges + BLOCKS * EDGES), I32),
            jax.ShapeDtypeStruct((PARTS, 3 + BLOCKS), I32),
        ),
        (embed_out, proj_grid, mesh_nodes, proj_mesh, node_self, keys),
        (),
        scratch=[weight] * 2 + [rows] + [weight] * 2 + [pltpu.SMEM((1, edges), I32), dma((7,))],
        out_specs=[pl.BlockSpec(memory_space=pltpu.VMEM)] * 4 + [pl.BlockSpec(memory_space=pltpu.SMEM)],
    )
    embed = jnp.pad(embed_in, ((0, WIDE - feats), (0, 0)))
    low, send_low, messages, line, weights = call(
        functools.partial(gather_kernel, feats),
        (
            rows_half,
            rows_half,
            pltpu.VMEM((slots, width), BF16),
            pltpu.VMEM((8, slots), F32),
            pltpu.VMEM((6 * width, width), BF16),
        ),
        (mesh_nodes, node_agg, edge_send, edge_recv, out_self, out_agg),
        (arrived, embed, fold, proj, own),
        scratch=[pltpu.VMEM((half, width), F32), dma((6,))],
    )

    forward = [(i, (i + 1) % faces) for i in range(faces)]
    backward = [(target, source) for source, target in forward]

    def neighbours(rows):
        return lax.ppermute(rows, "face", backward), lax.ppermute(rows, "face", forward)

    near = neighbours(send_low)
    acc, recv, own, high, send_high = call(
        own_kernel,
        (sums, pltpu.VMEM((mesh_rows + SPAN, width), BF16), rows_wide, rows_half, rows_half),
        (),
        (keys, low, send_low, messages, line, own, weights),
        scratch=[rows],
        smem=(plan,),
    )
    far = neighbours(send_high)
    acc = call(
        near_kernel,
        sums,
        (),
        (acc, keys, *near, recv),
        scratch=[rows],
        smem=(plan,),
        aliases={1: 0},
    )
    out, _ = call(
        far_kernel,
        (jax.ShapeDtypeStruct((mesh_rows, width), F32), sums),
        (),
        (acc, keys, *far, weights, recv, low, high, own),
        scratch=[rows, rows_wide, dma((4,))],
        out_specs=(there, pl.BlockSpec(memory_space=pltpu.VMEM)),
        smem=(plan,),
        aliases={1: 1},
    )
    return out


def solution(mesh):
    split = P(("band", "face"), None)
    return jax.shard_map(
        body,
        mesh=mesh,
        in_specs=(split,) * 7 + (P(),) * 10,
        out_specs=split,
        check_vma=False,
    )
```

```python
import functools

import jax
import jax.numpy as jnp
from jax import lax
from jax.experimental import pallas as pl
from jax.experimental.pallas import tpu as pltpu
from jax.sharding import PartitionSpec as P

BF16 = jnp.bfloat16
F32 = jnp.float32
I32 = jnp.int32
WIDE = 256
DEAD = 1024
SLOTS = 1024
ARRIVED = 1024
BLOCKS = 3
EDGES = 512
PARTS = 3
FEW = 256
SPAN = 256
ALIGN = 16
VMEM_BYTES = 40 * 1024 * 1024


def dot(a, b):
    return jnp.dot(a, b, preferred_element_type=F32)


def dot_rows(a, b):
    return lax.dot_general(a, b, (((1,), (1,)), ((), ())), preferred_element_type=F32)


def silu(v):
    half = 0.5 * v
    return half + half * jnp.tanh(half)


def one_hot(hit):
    return jnp.where(hit, 1.0, 0.0).astype(BF16)


def iota(shape, dim):
    return lax.broadcasted_iota(I32, shape, dim)


def receiver_code(receiver):
    return jnp.where(receiver <= DEAD // 4, receiver, DEAD // 4 - receiver)


def as_column(row):
    return jnp.broadcast_to(row, (8, row.shape[1])).T[:, 0:1]


def part(ref, index):
    rows = ref.shape[1]
    return ref.at[index * rows : (index + 1) * rows, :]


def start_copies(pairs, sems):
    copies = [
        pltpu.make_async_copy(source, target, sems.at[i]) for i, (source, target) in enumerate(pairs)
    ]
    for copy in copies:
        copy.start()
    return copies


def call(kernel, outs, hbm, vmem, scratch=(), out_specs=None, smem=(), aliases=None):
    def spec(space):
        return pl.BlockSpec(memory_space=space)

    if out_specs is None:
        out_specs = jax.tree.map(lambda _: spec(pltpu.VMEM), outs)
    args = list(smem)
    args += [pltpu.with_memory_space_constraint(arg, pltpu.HBM) for arg in hbm]
    args += [pltpu.with_memory_space_constraint(arg, pltpu.VMEM) for arg in vmem]
    spaces = [pltpu.SMEM] * len(smem) + [pltpu.HBM] * len(hbm) + [pltpu.VMEM] * len(vmem)
    return pl.pallas_call(
        kernel,
        out_shape=outs,
        in_specs=[spec(space) for space in spaces],
        out_specs=out_specs,
        scratch_shapes=list(scratch),
        input_output_aliases=aliases or {},
        compiler_params=pltpu.CompilerParams(vmem_limit_bytes=VMEM_BYTES),
    )(*args)


def pack_kernel(
    mesh_rows,
    feat_hbm,
    sender_hbm,
    receiver_hbm,
    count_hbm,
    from_hbm,
    to_hbm,
    out_hbm,
    key_hbm,
    feat_ref,
    sender_ref,
    receiver_ref,
    count_ref,
    from_ref,
    to_ref,
    column_ref,
    pad_ref,
    out_ref,
    key_ref,
    in_sem,
    feat_sem,
    out_sem,
    key_sem,
):
    feats, rows = feat_ref.shape
    slots = sender_ref.shape[1]
    owners = count_ref.shape[1]
    cap = slots // owners
    half = mesh_rows // 2
    small = start_copies(
        (
            (sender_hbm, sender_ref),
            (receiver_hbm, receiver_ref),
            (count_hbm, count_ref),
            (from_hbm, from_ref),
            (to_hbm, to_ref),
        ),
        in_sem,
    )
    pieces = feat_sem.shape[0]
    piece = rows // pieces
    cuts = [slice(i * piece, (i + 1) * piece) for i in range(pieces)]
    large = start_copies([(feat_hbm.at[:, cut], feat_ref.at[:, cut]) for cut in cuts], feat_sem)
    for copy in small:
        copy.wait()
    source = from_ref[...]
    row = lax.rem(source, mesh_rows)
    second = row // half
    mine = (source >= mesh_rows) & (source < 2 * mesh_rows)
    side = jnp.where(source < mesh_rows, half, 0)
    part = jnp.where(mine, 0, 1 + second)
    place = jnp.where(mine, row, row - second * half + side)
    key_ref[...] = (part * mesh_rows + to_ref[...]) * mesh_rows + place
    key_copy = pltpu.make_async_copy(key_ref, key_hbm, key_sem)
    key_copy.start()
    counts = jnp.broadcast_to(count_ref[...].astype(F32).astype(BF16), (8, owners))
    slot = iota((owners, slots), 1)
    first = iota((owners, slots), 0) * cap
    count = dot(counts, one_hot((slot >= first) & (slot < first + cap))).astype(I32)
    live = lax.rem(iota((8, slots), 1), cap) < count
    receiver = jnp.broadcast_to(receiver_ref[...], (8, slots))
    sender = jnp.broadcast_to(sender_ref[...], (8, slots))
    code = jnp.where(live, receiver_code(receiver), DEAD)
    column_ref[...] = jnp.where(iota((8, slots), 0) == 0, sender, code).T
    for copy in large:
        copy.wait()
    whole = feats // ALIGN * ALIGN
    pad_ref[:whole, :] = feat_ref[:whole, :]
    line = iota((WIDE - whole, rows), 0)
    rest = jnp.zeros((WIDE - whole, rows), F32)
    for i in range(whole, feats):
        rest = jnp.where(line == i - whole, feat_ref[i : i + 1, :].astype(F32), rest)
    pad_ref[whole:, :] = rest.astype(BF16)

    def leave(block):
        here = pl.ds(pl.multiple_of(block * SLOTS, SLOTS), SLOTS)
        return pltpu.make_async_copy(out_ref.at[here, :], out_hbm.at[here, :], out_sem.at[block])

    def step(block, carry):
        start = pl.multiple_of(block * SLOTS, SLOTS)
        here = pl.ds(start, SLOTS)
        columns = column_ref[here, :]
        picker = one_hot(columns[:, 0:1] == iota((SLOTS, rows), 1))
        column = iota((SLOTS, WIDE), 1)
        code = jnp.where(column == feats, columns[:, 1:2], 0).astype(F32)
        out_ref[here, :] = (dot_rows(picker, pad_ref[...]) + code).astype(BF16)
        leave(block).start()
        return carry

    lax.fori_loop(0, slots // SLOTS, step, 0)
    for block in range(slots // SLOTS):
        leave(block).wait()
    key_copy.wait()


def weights_kernel(
    embed_out_hbm,
    proj_grid_hbm,
    mesh_hbm,
    proj_mesh_hbm,
    node_self_hbm,
    key_hbm,
    fold_ref,
    proj_ref,
    self_ref,
    key_ref,
    plan_ref,
    embed_out_ref,
    proj_grid_ref,
    mesh_ref,
    proj_mesh_ref,
    node_self_ref,
    key_scalar,
    sems,
):
    edges = key_hbm.shape[1]
    pairs = (
        (embed_out_hbm, embed_out_ref),
        (proj_grid_hbm, proj_grid_ref),
        (mesh_hbm, mesh_ref),
        (proj_mesh_hbm, proj_mesh_ref),
        (node_self_hbm, node_self_ref),
        (key_hbm, key_ref.at[:, :edges]),
        (key_hbm, key_scalar),
    )
    copies = start_copies(pairs, sems)
    key_ref[:, edges:] = jnp.full((1, key_ref.shape[1] - edges), -1, I32)
    for copy in copies:
        copy.wait()
    plan_edges(key_scalar, plan_ref, mesh_ref.shape[0])
    fold_ref[...] = dot(embed_out_ref[...], proj_grid_ref[...]).astype(BF16)
    mesh = mesh_ref[...]
    proj_ref[...] = dot(mesh, proj_mesh_ref[...]).astype(BF16)
    self_ref[...] = dot(mesh, node_self_ref[...])


def next_rows(sums, own, mesh, node_agg):
    inner = own + dot(sums.astype(BF16), node_agg)
    return (mesh.astype(F32) + silu(inner)).astype(BF16)


def gather_kernel(
    feats,
    mesh_hbm,
    node_agg_hbm,
    edge_send_hbm,
    edge_recv_hbm,
    out_self_hbm,
    out_agg_hbm,
    x_ref,
    embed_ref,
    fold_ref,
    proj_ref,
    self_ref,
    low_ref,
    send_ref,
    msg_ref,
    line_ref,
    weight_ref,
    sum_ref,
    sems,
):
    sources = (edge_send_hbm, edge_recv_hbm, out_self_hbm, out_agg_hbm, node_agg_hbm, mesh_hbm)
    copies = start_copies([(hbm, part(weight_ref, i)) for i, hbm in enumerate(sources)], sems)
    slots = x_ref.shape[0]
    mesh_rows = self_ref.shape[0]
    half = mesh_rows // 2
    lanes = feats // 128 * 128
    along = one_hot(iota((8, WIDE - lanes), 1) == feats - lanes)
    sum_ref[...] = jnp.zeros_like(sum_ref)

    def step(block, carry):
        here = pl.ds(pl.multiple_of(block * ARRIVED, ARRIVED), ARRIVED)
        x = x_ref[here, :]
        hidden = silu(dot(x, embed_ref[...])).astype(BF16)
        column = x[:, feats : feats + 1].astype(F32)
        codes = receiver_code(iota((ARRIVED, mesh_rows), 1)).astype(F32)
        picker = one_hot(column == codes)
        message = silu(dot(hidden, fold_ref[...]) + dot(picker, proj_ref[...])).astype(BF16)
        msg_ref[here, :] = message
        line = dot_rows(along, x[:, lanes:])
        line_ref[:, here] = line
        codes = receiver_code(iota((half, ARRIVED), 0)).astype(F32)
        sum_ref[...] += dot(one_hot(line[0:1, :] == codes), message)
        return carry

    lax.fori_loop(0, slots // ARRIVED, step, 0)
    for copy in copies:
        copy.wait()
    mesh = part(weight_ref, 5)[:half, :]
    low_ref[...] = next_rows(sum_ref[...], self_ref[:half, :], mesh, part(weight_ref, 4)[...])
    send_ref[...] = dot(low_ref[...], part(weight_ref, 0)[...]).astype(BF16)


def plan_edges(key_scalar, plan_ref, mesh_rows):
    edges = key_scalar.shape[1]

    def first_at_least(limit):
        def halve(_, ends):
            low, high = ends
            middle = (low + high) // 2
            below = key_scalar[0, jnp.minimum(middle, edges - 1)] < limit
            go = low < high
            return (
                jnp.where(go & below, middle + 1, low),
                jnp.where(go & jnp.logical_not(below), middle, high),
            )

        ends = (jnp.int32(0), jnp.int32(edges))
        return lax.fori_loop(0, edges.bit_length(), halve, ends)[0]

    first = jnp.int32(0)
    for index in range(PARTS):
        last = jnp.int32(edges)
        if index < PARTS - 1:
            last = first_at_least((index + 1) * mesh_rows * mesh_rows)
        origin = first // 128 * 128

        def receiver_at(place):
            key = key_scalar[0, jnp.clip(place, 0, edges - 1)]
            return key // mesh_rows - index * mesh_rows

        narrow = jnp.bool_(True)
        for block in range(BLOCKS):
            start = origin + block * EDGES
            low = receiver_at(jnp.maximum(start, first))
            high = receiver_at(jnp.minimum(start + EDGES, last) - 1)
            empty = start >= last
            base = jnp.where(empty, 0, low // ALIGN * ALIGN)
            narrow = narrow & (empty | (high - base < SPAN))
            plan_ref[index, 3 + block] = base
        plan_ref[index, 0] = origin
        plan_ref[index, 1] = last
        plan_ref[index, 2] = narrow.astype(I32)
        first = last


def edge_sums(index, plan_ref, key_ref, table_ref, recv_ref, acc_ref):
    mesh_rows = table_ref.shape[0]
    origin = plan_ref[index, 0]
    last = plan_ref[index, 1]
    narrow = plan_ref[index, 2] == 1

    def split(start, count):
        keys = key_ref[:, pl.ds(pl.multiple_of(start, 128), count)]
        column = as_column(keys)
        place = column & (mesh_rows - 1)
        receiver = lax.div(column, mesh_rows) - index * mesh_rows
        line = lax.div(keys, mesh_rows) - index * mesh_rows
        line = jnp.where((keys < 0) | (line < 0) | (line >= mesh_rows), -mesh_rows, line)
        return place, receiver, line

    @pl.when(narrow)
    def _():
        for block in range(BLOCKS):
            base = pl.multiple_of(plan_ref[index, 3 + block], ALIGN)
            place, receiver, line = split(origin + block * EDGES, EDGES)
            from_table = one_hot(place == iota((EDGES, mesh_rows), 1))
            from_recv = one_hot(receiver - base == iota((EDGES, SPAN), 1))
            reach = pl.ds(base, SPAN)
            message = silu(dot(from_table, table_ref[...]) + dot(from_recv, recv_ref[reach, :]))
            selector = one_hot(line - base == iota((SPAN, EDGES), 0))
            acc_ref[reach, :] += dot(selector, message.astype(BF16))
    def general(block, carry):
        place, receiver, line = split(origin + block * FEW, FEW)
        from_table = one_hot(place == iota((FEW, mesh_rows), 1))
        from_recv = one_hot(receiver == iota((FEW, mesh_rows), 1))
        message = silu(dot(from_table, table_ref[...]) + dot(from_recv, recv_ref[:mesh_rows, :]))
        selector = one_hot(line == iota((mesh_rows, FEW), 0))
        acc_ref[:mesh_rows, :] += dot(selector, message.astype(BF16))
        return carry

    done = jnp.where(narrow, BLOCKS * EDGES // FEW, 0)
    lax.fori_loop(done, (last - origin + FEW - 1) // FEW, general, 0)


def high_kernel(
    low_ref,
    send_low_ref,
    msg_ref,
    line_ref,
    self_ref,
    weight_ref,
    high_ref,
    send_high_ref,
    table_ref,
    recv_ref,
    own_ref,
):
    half, width = low_ref.shape
    mesh_rows = 2 * half
    codes = receiver_code(iota((half, msg_ref.shape[0]), 0) + half).astype(F32)
    sums = dot(one_hot(line_ref[0:1, :] == codes), msg_ref[...])
    mesh = part(weight_ref, 5)[half:, :]
    high_ref[...] = next_rows(sums, self_ref[half:, :], mesh, part(weight_ref, 4)[...])
    send_high_ref[...] = dot(high_ref[...], part(weight_ref, 0)[...]).astype(BF16)
    table_ref[:half, :] = send_low_ref[...]
    table_ref[half:, :] = send_high_ref[...]
    recv_ref[mesh_rows:, :] = jnp.zeros((SPAN, width), BF16)
    for start, mid_ref in ((0, low_ref), (half, high_ref)):
        here = slice(start, start + half)
        mid = mid_ref[...]
        recv_ref[here, :] = dot(mid, part(weight_ref, 1)[...]).astype(BF16)
        own_ref[here, :] = dot(mid, part(weight_ref, 2)[...])


def own_kernel(plan_ref, key_ref, table_ref, recv_ref, acc_ref):
    acc_ref[...] = jnp.zeros_like(acc_ref)
    edge_sums(0, plan_ref, key_ref, table_ref, recv_ref, acc_ref)


def near_kernel(plan_ref, acc_in_ref, key_ref, right_ref, left_ref, recv_ref, acc_ref, table_ref):
    half = table_ref.shape[0] // 2
    table_ref[:half, :] = right_ref[...]
    table_ref[half:, :] = left_ref[...]
    edge_sums(1, plan_ref, key_ref, table_ref, recv_ref, acc_ref)


def far_kernel(
    plan_ref,
    acc_in_ref,
    key_ref,
    right_ref,
    left_ref,
    weight_ref,
    recv_ref,
    low_ref,
    high_ref,
    own_ref,
    out_hbm,
    acc_ref,
    table_ref,
    out_ref,
    sems,
):
    mesh_rows = table_ref.shape[0]
    half = mesh_rows // 2
    table_ref[:half, :] = right_ref[...]
    table_ref[half:, :] = left_ref[...]
    edge_sums(2, plan_ref, key_ref, table_ref, recv_ref, acc_ref)
    copies = []
    rows = mesh_rows // sems.shape[0]
    for index in range(sems.shape[0]):
        start = index * rows
        here = slice(start, start + rows)
        update = own_ref[here, :] + dot(acc_ref[here, :].astype(BF16), part(weight_ref, 3)[...])
        mid_ref = low_ref if start < half else high_ref
        mid = mid_ref[start % half : start % half + rows, :]
        values = mid.astype(F32) + silu(update)
        mean = jnp.mean(values, axis=-1, keepdims=True)
        centered = values - mean
        variance = jnp.mean(centered * centered, axis=-1, keepdims=True)
        out_ref[here, :] = centered * lax.rsqrt(variance + 1e-05)
        copies += start_copies([(out_ref.at[here, :], out_hbm.at[here, :])], sems.at[index : index + 1])
    for copy in copies:
        copy.wait()


def body(
    grid_feat,
    mesh_nodes,
    g2m_sender,
    g2m_receiver,
    send_counts,
    edge_sender,
    edge_receiver,
    embed_in,
    embed_out,
    proj_grid,
    proj_mesh,
    node_self,
    node_agg,
    edge_send,
    edge_recv,
    out_self,
    out_agg,
):
    owners = lax.axis_size(("band", "face"))
    faces = lax.axis_size("face")
    slots = g2m_sender.shape[1]
    grid_rows, feats = grid_feat.shape
    edges = edge_sender.shape[1]
    mesh_rows, width = mesh_nodes.shape
    half = mesh_rows // 2
    there = pl.BlockSpec(memory_space=pltpu.HBM)
    dma = pltpu.SemaphoreType.DMA
    weight = pltpu.VMEM((width, width), BF16)
    rows = pltpu.VMEM((mesh_rows, width), BF16)
    rows_half = pltpu.VMEM((half, width), BF16)
    rows_wide = pltpu.VMEM((mesh_rows, width), F32)
    sums = pltpu.VMEM((mesh_rows + SPAN, width), F32)

    packed, keys = call(
        functools.partial(pack_kernel, mesh_rows),
        (jax.ShapeDtypeStruct((slots, WIDE), BF16), jax.ShapeDtypeStruct((1, edges), I32)),
        (grid_feat.T, g2m_sender, g2m_receiver, send_counts, edge_sender, edge_receiver),
        (),
        scratch=[
            pltpu.VMEM((feats, grid_rows), BF16),
            pltpu.VMEM((1, slots), I32),
            pltpu.VMEM((1, slots), I32),
            pltpu.VMEM((1, owners), I32),
            pltpu.VMEM((1, edges), I32),
            pltpu.VMEM((1, edges), I32),
            pltpu.VMEM((slots, 8), I32),
            pltpu.VMEM((WIDE, grid_rows), BF16),
            pltpu.VMEM((slots, WIDE), BF16),
            pltpu.VMEM((1, edges), I32),
            dma((5,)),
            dma((1,)),
            dma((slots // SLOTS,)),
            dma,
        ],
        out_specs=(there, there),
    )
    keys = lax.sort(keys.reshape(edges), is_stable=False).reshape(1, edges)
    arrived = lax.all_to_all(
        packed.reshape(owners, slots // owners, WIDE),
        ("band", "face"),
        split_axis=0,
        concat_axis=0,
        tiled=True,
    ).reshape(slots, WIDE)
    fold, proj, own, keys, plan = call(
        weights_kernel,
        (
            weight,
            rows,
            rows_wide,
            pltpu.VMEM((1, edges + BLOCKS * EDGES), I32),
            jax.ShapeDtypeStruct((PARTS, 3 + BLOCKS), I32),
        ),
        (embed_out, proj_grid, mesh_nodes, proj_mesh, node_self, keys),
        (),
        scratch=[weight] * 2 + [rows] + [weight] * 2 + [pltpu.SMEM((1, edges), I32), dma((7,))],
        out_specs=[pl.BlockSpec(memory_space=pltpu.VMEM)] * 4 + [pl.BlockSpec(memory_space=pltpu.SMEM)],
    )
    embed = jnp.pad(embed_in, ((0, WIDE - feats), (0, 0)))
    low, send_low, messages, line, weights = call(
        functools.partial(gather_kernel, feats),
        (
            rows_half,
            rows_half,
            pltpu.VMEM((slots, width), BF16),
            pltpu.VMEM((8, slots), F32),
            pltpu.VMEM((6 * width, width), BF16),
        ),
        (mesh_nodes, node_agg, edge_send, edge_recv, out_self, out_agg),
        (arrived, embed, fold, proj, own),
        scratch=[pltpu.VMEM((half, width), F32), dma((6,))],
    )

    forward = [(i, (i + 1) % faces) for i in range(faces)]
    backward = [(target, source) for source, target in forward]

    def neighbours(rows):
        return lax.ppermute(rows, "face", backward), lax.ppermute(rows, "face", forward)

    near = neighbours(send_low)
    high, send_high, table, recv, own = call(
        high_kernel,
        (rows_half, rows_half, rows, pltpu.VMEM((mesh_rows + SPAN, width), BF16), rows_wide),
        (),
        (low, send_low, messages, line, own, weights),
    )
    far = neighbours(send_high)
    acc = call(own_kernel, sums, (), (keys, table, recv), smem=(plan,))
    acc = call(
        near_kernel,
        sums,
        (),
        (acc, keys, *near, recv),
        scratch=[rows],
        smem=(plan,),
        aliases={1: 0},
    )
    out, _ = call(
        far_kernel,
        (jax.ShapeDtypeStruct((mesh_rows, width), F32), sums),
        (),
        (acc, keys, *far, weights, recv, low, high, own),
        scratch=[rows, rows_wide, dma((4,))],
        out_specs=(there, pl.BlockSpec(memory_space=pltpu.VMEM)),
        smem=(plan,),
        aliases={1: 1},
    )
    return out


def solution(mesh):
    split = P(("band", "face"), None)
    return jax.shard_map(
        body,
        mesh=mesh,
        in_specs=(split,) * 7 + (P(),) * 10,
        out_specs=split,
        check_vma=False,
    )
```

```python
import functools

import jax
import jax.numpy as jnp
from jax import lax
from jax.experimental import pallas as pl
from jax.experimental.pallas import tpu as pltpu
from jax.sharding import PartitionSpec as P

BF16 = jnp.bfloat16
F32 = jnp.float32
I32 = jnp.int32
WIDE = 256
DEAD = 1024
SLOTS = 1024
ARRIVED = 1024
PARTS = 6
BLOCKS = 3
EDGES = 256
SPAN = 256
ALIGN = 16
VMEM_BYTES = 40 * 1024 * 1024


def dot(a, b):
    return jnp.dot(a, b, preferred_element_type=F32)


def dot_rows(a, b):
    return lax.dot_general(a, b, (((1,), (1,)), ((), ())), preferred_element_type=F32)


def silu(v):
    half = 0.5 * v
    return half + half * jnp.tanh(half)


def one_hot(hit):
    return jnp.where(hit, 1.0, 0.0).astype(BF16)


def iota(shape, dim):
    return lax.broadcasted_iota(I32, shape, dim)


def receiver_code(receiver):
    return jnp.where(receiver <= DEAD // 4, receiver, DEAD // 4 - receiver)


def as_column(row):
    return jnp.broadcast_to(row, (8, row.shape[1])).T[:, 0:1]


def part(ref, index):
    rows = ref.shape[1]
    return ref.at[index * rows : (index + 1) * rows, :]


def start_copies(pairs, sems):
    copies = [
        pltpu.make_async_copy(source, target, sems.at[i]) for i, (source, target) in enumerate(pairs)
    ]
    for copy in copies:
        copy.start()
    return copies


def call(kernel, outs, hbm, vmem, scratch=(), out_specs=None, smem=(), aliases=None):
    def spec(space):
        return pl.BlockSpec(memory_space=space)

    if out_specs is None:
        out_specs = jax.tree.map(lambda _: spec(pltpu.VMEM), outs)
    args = list(smem)
    args += [pltpu.with_memory_space_constraint(arg, pltpu.HBM) for arg in hbm]
    args += [pltpu.with_memory_space_constraint(arg, pltpu.VMEM) for arg in vmem]
    spaces = [pltpu.SMEM] * len(smem) + [pltpu.HBM] * len(hbm) + [pltpu.VMEM] * len(vmem)
    return pl.pallas_call(
        kernel,
        out_shape=outs,
        in_specs=[spec(space) for space in spaces],
        out_specs=out_specs,
        scratch_shapes=list(scratch),
        input_output_aliases=aliases or {},
        compiler_params=pltpu.CompilerParams(vmem_limit_bytes=VMEM_BYTES),
    )(*args)


def pack_kernel(
    mesh_rows,
    feat_hbm,
    sender_hbm,
    receiver_hbm,
    count_hbm,
    from_hbm,
    to_hbm,
    out_hbm,
    key_hbm,
    feat_ref,
    sender_ref,
    receiver_ref,
    count_ref,
    from_ref,
    to_ref,
    column_ref,
    pad_ref,
    out_ref,
    key_ref,
    in_sem,
    feat_sem,
    out_sem,
    key_sem,
):
    feats, rows = feat_ref.shape
    slots = sender_ref.shape[1]
    owners = count_ref.shape[1]
    cap = slots // owners
    half = mesh_rows // 2
    small = start_copies(
        (
            (sender_hbm, sender_ref),
            (receiver_hbm, receiver_ref),
            (count_hbm, count_ref),
            (from_hbm, from_ref),
            (to_hbm, to_ref),
        ),
        in_sem,
    )
    pieces = feat_sem.shape[0]
    piece = rows // pieces
    cuts = [slice(i * piece, (i + 1) * piece) for i in range(pieces)]
    large = start_copies([(feat_hbm.at[:, cut], feat_ref.at[:, cut]) for cut in cuts], feat_sem)
    for copy in small:
        copy.wait()
    source = from_ref[...]
    row = lax.rem(source, mesh_rows)
    second = row // half
    mine = (source >= mesh_rows) & (source < 2 * mesh_rows)
    left = (source < mesh_rows).astype(I32)
    part = jnp.where(mine, second, 2 + 2 * second + left)
    place = row - second * half
    key_ref[...] = (part * mesh_rows + to_ref[...]) * half + place
    key_copy = pltpu.make_async_copy(key_ref, key_hbm, key_sem)
    key_copy.start()
    counts = jnp.broadcast_to(count_ref[...].astype(F32).astype(BF16), (8, owners))
    slot = iota((owners, slots), 1)
    first = iota((owners, slots), 0) * cap
    count = dot(counts, one_hot((slot >= first) & (slot < first + cap))).astype(I32)
    live = lax.rem(iota((8, slots), 1), cap) < count
    receiver = jnp.broadcast_to(receiver_ref[...], (8, slots))
    sender = jnp.broadcast_to(sender_ref[...], (8, slots))
    code = jnp.where(live, receiver_code(receiver), DEAD)
    column_ref[...] = jnp.where(iota((8, slots), 0) == 0, sender, code).T
    for copy in large:
        copy.wait()
    whole = feats // ALIGN * ALIGN
    pad_ref[:whole, :] = feat_ref[:whole, :]
    line = iota((WIDE - whole, rows), 0)
    rest = jnp.zeros((WIDE - whole, rows), F32)
    for i in range(whole, feats):
        rest = jnp.where(line == i - whole, feat_ref[i : i + 1, :].astype(F32), rest)
    pad_ref[whole:, :] = rest.astype(BF16)

    def leave(block):
        here = pl.ds(pl.multiple_of(block * SLOTS, SLOTS), SLOTS)
        return pltpu.make_async_copy(out_ref.at[here, :], out_hbm.at[here, :], out_sem.at[block])

    def step(block, carry):
        start = pl.multiple_of(block * SLOTS, SLOTS)
        here = pl.ds(start, SLOTS)
        columns = column_ref[here, :]
        picker = one_hot(columns[:, 0:1] == iota((SLOTS, rows), 1))
        column = iota((SLOTS, WIDE), 1)
        code = jnp.where(column == feats, columns[:, 1:2], 0).astype(F32)
        out_ref[here, :] = (dot_rows(picker, pad_ref[...]) + code).astype(BF16)
        leave(block).start()
        return carry

    lax.fori_loop(0, slots // SLOTS, step, 0)
    for block in range(slots // SLOTS):
        leave(block).wait()
    key_copy.wait()


def weights_kernel(
    embed_out_hbm,
    proj_grid_hbm,
    mesh_hbm,
    proj_mesh_hbm,
    node_self_hbm,
    key_hbm,
    fold_ref,
    proj_ref,
    self_ref,
    key_ref,
    line_ref,
    column_ref,
    plan_ref,
    embed_out_ref,
    proj_grid_ref,
    mesh_ref,
    proj_mesh_ref,
    node_self_ref,
    place_ref,
    key_scalar,
    sems,
):
    edges = key_hbm.shape[1]
    pairs = (
        (embed_out_hbm, embed_out_ref),
        (proj_grid_hbm, proj_grid_ref),
        (mesh_hbm, mesh_ref),
        (proj_mesh_hbm, proj_mesh_ref),
        (node_self_hbm, node_self_ref),
        (key_hbm, key_ref.at[:, :edges]),
        (key_hbm, key_scalar),
    )
    copies = start_copies(pairs, sems)
    key_ref[:, edges:] = jnp.full((1, key_ref.shape[1] - edges), -1, I32)
    for copy in copies:
        copy.wait()
    plan_edges(key_scalar, key_ref, plan_ref, line_ref, place_ref, column_ref, mesh_ref.shape[0])
    fold_ref[...] = dot(embed_out_ref[...], proj_grid_ref[...]).astype(BF16)
    mesh = mesh_ref[...]
    proj_ref[...] = dot(mesh, proj_mesh_ref[...]).astype(BF16)
    self_ref[...] = dot(mesh, node_self_ref[...])


def next_rows(sums, own, mesh, node_agg):
    inner = own + dot(sums.astype(BF16), node_agg)
    return (mesh.astype(F32) + silu(inner)).astype(BF16)


def gather_kernel(
    feats,
    mesh_hbm,
    node_agg_hbm,
    edge_send_hbm,
    edge_recv_hbm,
    out_self_hbm,
    out_agg_hbm,
    x_ref,
    embed_ref,
    fold_ref,
    proj_ref,
    self_ref,
    low_ref,
    send_ref,
    msg_ref,
    line_ref,
    weight_ref,
    sum_ref,
    sems,
):
    sources = (edge_send_hbm, edge_recv_hbm, out_self_hbm, out_agg_hbm, node_agg_hbm, mesh_hbm)
    copies = start_copies([(hbm, part(weight_ref, i)) for i, hbm in enumerate(sources)], sems)
    slots = x_ref.shape[0]
    mesh_rows = self_ref.shape[0]
    early = low_ref.shape[0]
    lanes = feats // 128 * 128
    along = one_hot(iota((8, WIDE - lanes), 1) == feats - lanes)
    sum_ref[...] = jnp.zeros_like(sum_ref)

    def step(block, carry):
        here = pl.ds(pl.multiple_of(block * ARRIVED, ARRIVED), ARRIVED)
        x = x_ref[here, :]
        hidden = silu(dot(x, embed_ref[...])).astype(BF16)
        column = x[:, feats : feats + 1].astype(F32)
        codes = receiver_code(iota((ARRIVED, mesh_rows), 1)).astype(F32)
        picker = one_hot(column == codes)
        message = silu(dot(hidden, fold_ref[...]) + dot(picker, proj_ref[...])).astype(BF16)
        msg_ref[here, :] = message
        line = dot_rows(along, x[:, lanes:])
        line_ref[:, here] = line
        codes = receiver_code(iota((early, ARRIVED), 0)).astype(F32)
        sum_ref[...] += dot(one_hot(line[0:1, :] == codes), message)
        return carry

    lax.fori_loop(0, slots // ARRIVED, step, 0)
    for copy in copies:
        copy.wait()
    mesh = part(weight_ref, 5)[:early, :]
    low_ref[...] = next_rows(sum_ref[...], self_ref[:early, :], mesh, part(weight_ref, 4)[...])
    send_ref[...] = dot(low_ref[...], part(weight_ref, 0)[...]).astype(BF16)


def plan_edges(key_scalar, key_ref, plan_ref, line_ref, place_ref, column_ref, mesh_rows):
    edges = key_scalar.shape[1]
    half = mesh_rows // 2

    def first_at_least(limit):
        def halve(_, ends):
            low, high = ends
            middle = (low + high) // 2
            below = key_scalar[0, jnp.minimum(middle, edges - 1)] < limit
            go = low < high
            return (
                jnp.where(go & below, middle + 1, low),
                jnp.where(go & jnp.logical_not(below), middle, high),
            )

        ends = (jnp.int32(0), jnp.int32(edges))
        return lax.fori_loop(0, edges.bit_length(), halve, ends)[0]

    first = jnp.int32(0)
    lines = []
    places = []
    for index in range(PARTS):
        last = jnp.int32(edges)
        if index < PARTS - 1:
            last = first_at_least((index + 1) * mesh_rows * half)
        share = (last - first + BLOCKS - 1) // BLOCKS

        def receiver_at(position):
            key = key_scalar[0, jnp.clip(position, 0, edges - 1)]
            return key // half - index * mesh_rows

        narrow = share <= EDGES
        for block in range(BLOCKS):
            start = jnp.minimum(first + block * share, last)
            end = jnp.minimum(start + share, last)
            empty = start >= end
            base = jnp.where(empty, 0, receiver_at(start) // ALIGN * ALIGN)
            narrow = narrow & (empty | (receiver_at(end - 1) - base < SPAN))
            plan_ref[index, 3 + block] = base
            begin = pl.multiple_of(start // 128 * 128, 128)
            width = EDGES + 128
            keys = jnp.broadcast_to(key_ref[:, pl.ds(begin, width)], (8, width))
            keys = pltpu.roll(keys, lax.rem(width - (start - begin), width), axis=1)[0:1, :EDGES]
            live = iota((1, EDGES), 1) < end - start
            receiver = lax.div(keys, half) - index * mesh_rows - base
            lines.append(jnp.where(live, receiver, -mesh_rows))
            places.append(keys & (half - 1))
        plan_ref[index, 0] = first
        plan_ref[index, 1] = last
        plan_ref[index, 2] = narrow.astype(I32)
        first = last
    rows = line_ref.shape[0]
    for block in range(PARTS * BLOCKS):
        line_ref[block : block + 1, :] = lines[block]
        place_ref[block : block + 1, :] = places[block]
    for block in range(PARTS * BLOCKS, rows):
        line_ref[block : block + 1, :] = jnp.full((1, EDGES), -mesh_rows, I32)
        place_ref[block : block + 1, :] = jnp.zeros((1, EDGES), I32)
    column_ref[:, :rows] = line_ref[...].T
    column_ref[:, rows:] = place_ref[...].T


def edge_sums(parts, plan_refs, recv_ref, acc_ref):
    plan_ref, key_ref, line_ref, column_ref = plan_refs
    half = parts[0][1].shape[0]
    mesh_rows = 2 * half
    rows = line_ref.shape[0]
    narrow = functools.reduce(jnp.logical_and, [plan_ref[index, 2] == 1 for index, _ in parts])

    @pl.when(narrow)
    def _():
        pending = []

        def scatter():
            row, reach, message = pending.pop(0)
            selector = one_hot(line_ref[row : row + 1, :] == iota((SPAN, EDGES), 0))
            acc_ref[reach, :] += dot(selector, message)

        for index, table in parts:
            for block in range(BLOCKS):
                row = index * BLOCKS + block
                reach = pl.ds(pl.multiple_of(plan_ref[index, 3 + block], ALIGN), SPAN)
                receiver = column_ref[:, row : row + 1]
                place = column_ref[:, rows + row : rows + row + 1]
                from_table = one_hot(place == iota((EDGES, half), 1))
                from_recv = one_hot(receiver == iota((EDGES, SPAN), 1))
                pre = dot(from_table, table[...]) + dot(from_recv, recv_ref[reach, :])
                if pending:
                    scatter()
                pending.append((row, reach, silu(pre).astype(BF16)))
        scatter()

    for index, table in parts:
        origin = plan_ref[index, 0] // 128 * 128

        def general(block, carry):
            keys = key_ref[:, pl.ds(pl.multiple_of(origin + block * EDGES, 128), EDGES)]
            column = as_column(keys)
            receiver = lax.div(column, half) - index * mesh_rows
            from_table = one_hot((column & (half - 1)) == iota((EDGES, half), 1))
            from_recv = one_hot(receiver == iota((EDGES, mesh_rows), 1))
            message = silu(dot(from_table, table[...]) + dot(from_recv, recv_ref[:mesh_rows, :]))
            line = lax.div(keys, half) - index * mesh_rows
            line = jnp.where((keys < 0) | (line < 0) | (line >= mesh_rows), -mesh_rows, line)
            selector = one_hot(line == iota((mesh_rows, EDGES), 0))
            acc_ref[:mesh_rows, :] += dot(selector, message.astype(BF16))
            return carry

        blocks = (plan_ref[index, 1] - origin + EDGES - 1) // EDGES
        lax.fori_loop(0, jnp.where(narrow, 0, blocks), general, 0)


def high_kernel(
    low_ref,
    send_low_ref,
    msg_ref,
    line_ref,
    self_ref,
    weight_ref,
    high_ref,
    send_high_ref,
    table_ref,
    recv_ref,
    own_ref,
):
    early, width = low_ref.shape
    late = high_ref.shape[0]
    mesh_rows = early + late
    codes = receiver_code(iota((late, msg_ref.shape[0]), 0) + early).astype(F32)
    sums = dot(one_hot(line_ref[0:1, :] == codes), msg_ref[...])
    mesh = part(weight_ref, 5)[early:, :]
    high_ref[...] = next_rows(sums, self_ref[early:, :], mesh, part(weight_ref, 4)[...])
    send_high_ref[...] = dot(high_ref[...], part(weight_ref, 0)[...]).astype(BF16)
    table_ref[:early, :] = send_low_ref[...]
    table_ref[early:, :] = send_high_ref[...]
    recv_ref[mesh_rows:, :] = jnp.zeros((SPAN, width), BF16)
    for start, mid_ref in ((0, low_ref), (early, high_ref)):
        here = slice(start, start + mid_ref.shape[0])
        mid = mid_ref[...]
        recv_ref[here, :] = dot(mid, part(weight_ref, 1)[...]).astype(BF16)
        own_ref[here, :] = dot(mid, part(weight_ref, 2)[...])


def own_kernel(plan_ref, key_ref, line_ref, column_ref, table_ref, recv_ref, acc_ref):
    half = table_ref.shape[0] // 2
    acc_ref[...] = jnp.zeros_like(acc_ref)
    parts = [(0, table_ref.at[:half, :]), (1, table_ref.at[half:, :])]
    edge_sums(parts, (plan_ref, key_ref, line_ref, column_ref), recv_ref, acc_ref)


def near_kernel(
    plan_ref, acc_in_ref, key_ref, line_ref, column_ref, right_ref, left_ref, recv_ref, acc_ref
):
    parts = [(2, right_ref), (3, left_ref)]
    edge_sums(parts, (plan_ref, key_ref, line_ref, column_ref), recv_ref, acc_ref)


def far_kernel(
    plan_ref,
    acc_in_ref,
    key_ref,
    line_ref,
    column_ref,
    right_ref,
    left_ref,
    weight_ref,
    recv_ref,
    low_ref,
    high_ref,
    own_ref,
    out_hbm,
    acc_ref,
    out_ref,
    sems,
):
    early = low_ref.shape[0]
    mesh_rows = early + high_ref.shape[0]
    parts = [(4, right_ref), (5, left_ref)]
    edge_sums(parts, (plan_ref, key_ref, line_ref, column_ref), recv_ref, acc_ref)
    copies = []
    rows = mesh_rows // sems.shape[0]
    for index in range(sems.shape[0]):
        start = index * rows
        here = slice(start, start + rows)
        update = own_ref[here, :] + dot(acc_ref[here, :].astype(BF16), part(weight_ref, 3)[...])
        mid = low_ref[here, :] if start < early else high_ref[start - early : start - early + rows, :]
        values = mid.astype(F32) + silu(update)
        mean = jnp.mean(values, axis=-1, keepdims=True)
        centered = values - mean
        variance = jnp.mean(centered * centered, axis=-1, keepdims=True)
        out_ref[here, :] = centered * lax.rsqrt(variance + 1e-05)
        copies += start_copies([(out_ref.at[here, :], out_hbm.at[here, :])], sems.at[index : index + 1])
    for copy in copies:
        copy.wait()


def body(
    grid_feat,
    mesh_nodes,
    g2m_sender,
    g2m_receiver,
    send_counts,
    edge_sender,
    edge_receiver,
    embed_in,
    embed_out,
    proj_grid,
    proj_mesh,
    node_self,
    node_agg,
    edge_send,
    edge_recv,
    out_self,
    out_agg,
):
    owners = lax.axis_size(("band", "face"))
    faces = lax.axis_size("face")
    slots = g2m_sender.shape[1]
    grid_rows, feats = grid_feat.shape
    edges = edge_sender.shape[1]
    mesh_rows, width = mesh_nodes.shape
    half = mesh_rows // 2
    there = pl.BlockSpec(memory_space=pltpu.HBM)
    dma = pltpu.SemaphoreType.DMA
    weight = pltpu.VMEM((width, width), BF16)
    rows = pltpu.VMEM((mesh_rows, width), BF16)
    rows_half = pltpu.VMEM((half, width), BF16)
    lines = pltpu.VMEM((PARTS * BLOCKS + -PARTS * BLOCKS % 8, EDGES), I32)
    columns = pltpu.VMEM((EDGES, 2 * lines.shape[0]), I32)
    rows_wide = pltpu.VMEM((mesh_rows, width), F32)
    sums = pltpu.VMEM((mesh_rows + SPAN, width), F32)

    packed, keys = call(
        functools.partial(pack_kernel, mesh_rows),
        (jax.ShapeDtypeStruct((slots, WIDE), BF16), jax.ShapeDtypeStruct((1, edges), I32)),
        (grid_feat.T, g2m_sender, g2m_receiver, send_counts, edge_sender, edge_receiver),
        (),
        scratch=[
            pltpu.VMEM((feats, grid_rows), BF16),
            pltpu.VMEM((1, slots), I32),
            pltpu.VMEM((1, slots), I32),
            pltpu.VMEM((1, owners), I32),
            pltpu.VMEM((1, edges), I32),
            pltpu.VMEM((1, edges), I32),
            pltpu.VMEM((slots, 8), I32),
            pltpu.VMEM((WIDE, grid_rows), BF16),
            pltpu.VMEM((slots, WIDE), BF16),
            pltpu.VMEM((1, edges), I32),
            dma((5,)),
            dma((1,)),
            dma((slots // SLOTS,)),
            dma,
        ],
        out_specs=(there, there),
    )
    keys = lax.sort(keys.reshape(edges), is_stable=False).reshape(1, edges)
    arrived = lax.all_to_all(
        packed.reshape(owners, slots // owners, WIDE),
        ("band", "face"),
        split_axis=0,
        concat_axis=0,
        tiled=True,
    ).reshape(slots, WIDE)
    fold, proj, own, keys, line, column, plan = call(
        weights_kernel,
        (
            weight,
            rows,
            rows_wide,
            pltpu.VMEM((1, edges + 2 * EDGES), I32),
            lines,
            columns,
            jax.ShapeDtypeStruct((PARTS, 3 + BLOCKS), I32),
        ),
        (embed_out, proj_grid, mesh_nodes, proj_mesh, node_self, keys),
        (),
        scratch=[weight] * 2 + [rows] + [weight] * 2 + [lines, pltpu.SMEM((1, edges), I32), dma((7,))],
        out_specs=[pl.BlockSpec(memory_space=pltpu.VMEM)] * 6 + [pl.BlockSpec(memory_space=pltpu.SMEM)],
    )
    embed = jnp.pad(embed_in, ((0, WIDE - feats), (0, 0)))
    low, send_low, messages, target, weights = call(
        functools.partial(gather_kernel, feats),
        (
            rows_half,
            rows_half,
            pltpu.VMEM((slots, width), BF16),
            pltpu.VMEM((8, slots), F32),
            pltpu.VMEM((6 * width, width), BF16),
        ),
        (mesh_nodes, node_agg, edge_send, edge_recv, out_self, out_agg),
        (arrived, embed, fold, proj, own),
        scratch=[pltpu.VMEM((half, width), F32), dma((6,))],
    )

    forward = [(i, (i + 1) % faces) for i in range(faces)]
    backward = [(target, source) for source, target in forward]

    def neighbours(rows):
        return lax.ppermute(rows, "face", backward), lax.ppermute(rows, "face", forward)

    near = neighbours(send_low)
    high, send_high, own_table, recv, own = call(
        high_kernel,
        (rows_half, rows_half, rows, pltpu.VMEM((mesh_rows + SPAN, width), BF16), rows_wide),
        (),
        (low, send_low, messages, target, own, weights),
    )
    far = neighbours(send_high)
    acc = call(own_kernel, sums, (), (keys, line, column, own_table, recv), smem=(plan,))
    acc = call(
        near_kernel,
        sums,
        (),
        (acc, keys, line, column, *near, recv),
        smem=(plan,),
        aliases={1: 0},
    )
    out, _ = call(
        far_kernel,
        (jax.ShapeDtypeStruct((mesh_rows, width), F32), sums),
        (),
        (acc, keys, line, column, *far, weights, recv, low, high, own),
        scratch=[rows_wide, dma((4,))],
        out_specs=(there, pl.BlockSpec(memory_space=pltpu.VMEM)),
        smem=(plan,),
        aliases={1: 1},
    )
    return out


def solution(mesh):
    split = P(("band", "face"), None)
    return jax.shard_map(
        body,
        mesh=mesh,
        in_specs=(split,) * 7 + (P(),) * 10,
        out_specs=split,
        check_vma=False,
    )
```

```python
import functools

import jax
import jax.numpy as jnp
from jax import lax
from jax.experimental import pallas as pl
from jax.experimental.pallas import tpu as pltpu
from jax.sharding import PartitionSpec as P

BF16 = jnp.bfloat16
F32 = jnp.float32
I32 = jnp.int32
WIDE = 256
DEAD = 1024
SLOTS = 2048
ARRIVED = 1024
PARTS = 6
BLOCKS = 3
EDGES = 256
SPAN = 256
ALIGN = 16
VMEM_BYTES = 40 * 1024 * 1024


def dot(a, b):
    return jnp.dot(a, b, preferred_element_type=F32)


def dot_rows(a, b):
    return lax.dot_general(a, b, (((1,), (1,)), ((), ())), preferred_element_type=F32)


def silu(v):
    half = 0.5 * v
    return half + half * jnp.tanh(half)


def one_hot(hit):
    return jnp.where(hit, 1.0, 0.0).astype(BF16)


def iota(shape, dim):
    return lax.broadcasted_iota(I32, shape, dim)


def receiver_code(receiver):
    return jnp.where(receiver <= DEAD // 4, receiver, DEAD // 4 - receiver)


def as_column(row):
    return jnp.broadcast_to(row, (8, row.shape[1])).T[:, 0:1]


def part(ref, index):
    rows = ref.shape[1]
    return ref.at[index * rows : (index + 1) * rows, :]


def start_copies(pairs, sems):
    copies = [
        pltpu.make_async_copy(source, target, sems.at[i]) for i, (source, target) in enumerate(pairs)
    ]
    for copy in copies:
        copy.start()
    return copies


def call(kernel, outs, hbm, vmem, scratch=(), out_specs=None, smem=(), aliases=None):
    def spec(space):
        return pl.BlockSpec(memory_space=space)

    if out_specs is None:
        out_specs = jax.tree.map(lambda _: spec(pltpu.VMEM), outs)
    args = list(smem)
    args += [pltpu.with_memory_space_constraint(arg, pltpu.HBM) for arg in hbm]
    args += [pltpu.with_memory_space_constraint(arg, pltpu.VMEM) for arg in vmem]
    spaces = [pltpu.SMEM] * len(smem) + [pltpu.HBM] * len(hbm) + [pltpu.VMEM] * len(vmem)
    return pl.pallas_call(
        kernel,
        out_shape=outs,
        in_specs=[spec(space) for space in spaces],
        out_specs=out_specs,
        scratch_shapes=list(scratch),
        input_output_aliases=aliases or {},
        compiler_params=pltpu.CompilerParams(vmem_limit_bytes=VMEM_BYTES),
    )(*args)


def pack_kernel(
    mesh_rows,
    feat_hbm,
    sender_hbm,
    receiver_hbm,
    count_hbm,
    from_hbm,
    to_hbm,
    out_hbm,
    key_hbm,
    feat_ref,
    sender_ref,
    receiver_ref,
    count_ref,
    from_ref,
    to_ref,
    column_ref,
    pad_ref,
    out_ref,
    key_ref,
    in_sem,
    feat_sem,
    out_sem,
    key_sem,
):
    feats, rows = feat_ref.shape
    slots = sender_ref.shape[1]
    owners = count_ref.shape[1]
    cap = slots // owners
    half = mesh_rows // 2
    small = start_copies(
        (
            (sender_hbm, sender_ref),
            (receiver_hbm, receiver_ref),
            (count_hbm, count_ref),
            (from_hbm, from_ref),
            (to_hbm, to_ref),
        ),
        in_sem,
    )
    pieces = feat_sem.shape[0]
    piece = rows // pieces
    cuts = [slice(i * piece, (i + 1) * piece) for i in range(pieces)]
    large = start_copies([(feat_hbm.at[:, cut], feat_ref.at[:, cut]) for cut in cuts], feat_sem)
    for copy in small:
        copy.wait()
    source = from_ref[...]
    row = lax.rem(source, mesh_rows)
    second = row // half
    mine = (source >= mesh_rows) & (source < 2 * mesh_rows)
    left = (source < mesh_rows).astype(I32)
    part = jnp.where(mine, second, 2 + 2 * second + left)
    place = row - second * half
    key_ref[...] = (part * mesh_rows + to_ref[...]) * half + place
    key_copy = pltpu.make_async_copy(key_ref, key_hbm, key_sem)
    key_copy.start()
    counts = jnp.broadcast_to(count_ref[...].astype(F32).astype(BF16), (8, owners))
    slot = iota((owners, slots), 1)
    first = iota((owners, slots), 0) * cap
    count = dot(counts, one_hot((slot >= first) & (slot < first + cap))).astype(I32)
    live = lax.rem(iota((8, slots), 1), cap) < count
    receiver = jnp.broadcast_to(receiver_ref[...], (8, slots))
    sender = jnp.broadcast_to(sender_ref[...], (8, slots))
    code = jnp.where(live, receiver_code(receiver), DEAD)
    column_ref[...] = jnp.where(iota((8, slots), 0) == 0, sender, code).T
    for copy in large:
        copy.wait()
    whole = feats // ALIGN * ALIGN
    pad_ref[:whole, :] = feat_ref[:whole, :]
    line = iota((WIDE - whole, rows), 0)
    rest = jnp.zeros((WIDE - whole, rows), F32)
    for i in range(whole, feats):
        rest = jnp.where(line == i - whole, feat_ref[i : i + 1, :].astype(F32), rest)
    pad_ref[whole:, :] = rest.astype(BF16)

    def leave(block):
        here = pl.ds(pl.multiple_of(block * SLOTS, SLOTS), SLOTS)
        return pltpu.make_async_copy(out_ref.at[here, :], out_hbm.at[here, :], out_sem.at[block])

    def step(block, carry):
        start = pl.multiple_of(block * SLOTS, SLOTS)
        here = pl.ds(start, SLOTS)
        columns = column_ref[here, :]
        picker = one_hot(columns[:, 0:1] == iota((SLOTS, rows), 1))
        column = iota((SLOTS, WIDE), 1)
        code = jnp.where(column == feats, columns[:, 1:2], 0).astype(F32)
        out_ref[here, :] = (dot_rows(picker, pad_ref[...]) + code).astype(BF16)
        leave(block).start()
        return carry

    lax.fori_loop(0, slots // SLOTS, step, 0)
    for block in range(slots // SLOTS):
        leave(block).wait()
    key_copy.wait()


def weights_kernel(
    embed_out_hbm,
    proj_grid_hbm,
    mesh_hbm,
    proj_mesh_hbm,
    node_self_hbm,
    key_hbm,
    fold_ref,
    proj_ref,
    self_ref,
    key_ref,
    line_ref,
    column_ref,
    plan_ref,
    embed_out_ref,
    proj_grid_ref,
    mesh_ref,
    proj_mesh_ref,
    node_self_ref,
    place_ref,
    key_scalar,
    sems,
):
    edges = key_hbm.shape[1]
    pairs = (
        (embed_out_hbm, embed_out_ref),
        (proj_grid_hbm, proj_grid_ref),
        (mesh_hbm, mesh_ref),
        (proj_mesh_hbm, proj_mesh_ref),
        (node_self_hbm, node_self_ref),
        (key_hbm, key_ref.at[:, :edges]),
        (key_hbm, key_scalar),
    )
    copies = start_copies(pairs, sems)
    key_ref[:, edges:] = jnp.full((1, key_ref.shape[1] - edges), -1, I32)
    for copy in copies:
        copy.wait()
    plan_edges(key_scalar, key_ref, plan_ref, line_ref, place_ref, column_ref, mesh_ref.shape[0])
    fold_ref[...] = dot(embed_out_ref[...], proj_grid_ref[...]).astype(BF16)
    mesh = mesh_ref[...]
    proj_ref[...] = dot(mesh, proj_mesh_ref[...]).astype(BF16)
    self_ref[...] = dot(mesh, node_self_ref[...])


def next_rows(sums, own, mesh, node_agg):
    inner = own + dot(sums.astype(BF16), node_agg)
    return (mesh.astype(F32) + silu(inner)).astype(BF16)


def gather_kernel(
    feats,
    mesh_hbm,
    node_agg_hbm,
    edge_send_hbm,
    edge_recv_hbm,
    out_self_hbm,
    out_agg_hbm,
    x_ref,
    embed_ref,
    fold_ref,
    proj_ref,
    self_ref,
    low_ref,
    send_ref,
    msg_ref,
    line_ref,
    weight_ref,
    sum_ref,
    sems,
):
    sources = (edge_send_hbm, edge_recv_hbm, out_self_hbm, out_agg_hbm, node_agg_hbm, mesh_hbm)
    copies = start_copies([(hbm, part(weight_ref, i)) for i, hbm in enumerate(sources)], sems)
    slots = x_ref.shape[0]
    mesh_rows = self_ref.shape[0]
    early = low_ref.shape[0]
    lanes = feats // 128 * 128
    along = one_hot(iota((8, WIDE - lanes), 1) == feats - lanes)
    sum_ref[...] = jnp.zeros_like(sum_ref)

    def step(block, carry):
        here = pl.ds(pl.multiple_of(block * ARRIVED, ARRIVED), ARRIVED)
        x = x_ref[here, :]
        hidden = silu(dot(x, embed_ref[...])).astype(BF16)
        column = x[:, feats : feats + 1].astype(F32)
        codes = receiver_code(iota((ARRIVED, mesh_rows), 1)).astype(F32)
        picker = one_hot(column == codes)
        message = silu(dot(hidden, fold_ref[...]) + dot(picker, proj_ref[...])).astype(BF16)
        msg_ref[here, :] = message
        line = dot_rows(along, x[:, lanes:])
        line_ref[:, here] = line
        codes = receiver_code(iota((early, ARRIVED), 0)).astype(F32)
        sum_ref[...] += dot(one_hot(line[0:1, :] == codes), message)
        return carry

    lax.fori_loop(0, slots // ARRIVED, step, 0)
    for copy in copies:
        copy.wait()
    mesh = part(weight_ref, 5)[:early, :]
    low_ref[...] = next_rows(sum_ref[...], self_ref[:early, :], mesh, part(weight_ref, 4)[...])
    send_ref[...] = dot(low_ref[...], part(weight_ref, 0)[...]).astype(BF16)


def plan_edges(key_scalar, key_ref, plan_ref, line_ref, place_ref, column_ref, mesh_rows):
    edges = key_scalar.shape[1]
    half = mesh_rows // 2

    def first_at_least(limit):
        def halve(_, ends):
            low, high = ends
            middle = (low + high) // 2
            below = key_scalar[0, jnp.minimum(middle, edges - 1)] < limit
            go = low < high
            return (
                jnp.where(go & below, middle + 1, low),
                jnp.where(go & jnp.logical_not(below), middle, high),
            )

        ends = (jnp.int32(0), jnp.int32(edges))
        return lax.fori_loop(0, edges.bit_length(), halve, ends)[0]

    first = jnp.int32(0)
    lines = []
    places = []
    for index in range(PARTS):
        last = jnp.int32(edges)
        if index < PARTS - 1:
            last = first_at_least((index + 1) * mesh_rows * half)
        share = (last - first + BLOCKS - 1) // BLOCKS

        def receiver_at(position):
            key = key_scalar[0, jnp.clip(position, 0, edges - 1)]
            return key // half - index * mesh_rows

        narrow = share <= EDGES
        for block in range(BLOCKS):
            start = jnp.minimum(first + block * share, last)
            end = jnp.minimum(start + share, last)
            empty = start >= end
            base = jnp.where(empty, 0, receiver_at(start) // ALIGN * ALIGN)
            narrow = narrow & (empty | (receiver_at(end - 1) - base < SPAN))
            plan_ref[index, 3 + block] = base
            begin = pl.multiple_of(start // 128 * 128, 128)
            width = EDGES + 128
            keys = jnp.broadcast_to(key_ref[:, pl.ds(begin, width)], (8, width))
            keys = pltpu.roll(keys, lax.rem(width - (start - begin), width), axis=1)[0:1, :EDGES]
            live = iota((1, EDGES), 1) < end - start
            receiver = lax.div(keys, half) - index * mesh_rows - base
            lines.append(jnp.where(live, receiver, -mesh_rows))
            places.append(keys & (half - 1))
        plan_ref[index, 0] = first
        plan_ref[index, 1] = last
        plan_ref[index, 2] = narrow.astype(I32)
        first = last
    rows = line_ref.shape[0]
    for block in range(PARTS * BLOCKS):
        line_ref[block : block + 1, :] = lines[block]
        place_ref[block : block + 1, :] = places[block]
    for block in range(PARTS * BLOCKS, rows):
        line_ref[block : block + 1, :] = jnp.full((1, EDGES), -mesh_rows, I32)
        place_ref[block : block + 1, :] = jnp.zeros((1, EDGES), I32)
    column_ref[:, :rows] = line_ref[...].T
    column_ref[:, rows:] = place_ref[...].T


def all_narrow(plan_ref, indices):
    return functools.reduce(jnp.logical_and, [plan_ref[index, 2] == 1 for index in indices])


def reach_of(plan_ref, index, block):
    return pl.ds(pl.multiple_of(plan_ref[index, 3 + block], ALIGN), SPAN)


def pick_receivers(index, block, plan_ref, column_ref, recv_ref):
    row = index * BLOCKS + block
    picker = one_hot(column_ref[:, row : row + 1] == iota((EDGES, SPAN), 1))
    return dot(picker, recv_ref[reach_of(plan_ref, index, block), :])


def edge_sums(parts, plan_refs, recv_ref, acc_ref, met_ref=None):
    plan_ref, key_ref, line_ref, column_ref = plan_refs
    half = parts[0][1].shape[0]
    mesh_rows = 2 * half
    rows = line_ref.shape[0]
    narrow = all_narrow(plan_ref, [index for index, _ in parts])

    @pl.when(narrow)
    def _():
        pending = []

        def scatter():
            row, reach, message = pending.pop(0)
            selector = one_hot(line_ref[row : row + 1, :] == iota((SPAN, EDGES), 0))
            acc_ref[reach, :] += dot(selector, message)

        for order, (index, table) in enumerate(parts):
            for block in range(BLOCKS):
                row = index * BLOCKS + block
                reach = reach_of(plan_ref, index, block)
                place = column_ref[:, rows + row : rows + row + 1]
                from_table = one_hot(place == iota((EDGES, half), 1))
                if met_ref is None:
                    met = pick_receivers(index, block, plan_ref, column_ref, recv_ref)
                else:
                    at = (order * BLOCKS + block) * EDGES
                    met = met_ref[at : at + EDGES, :]
                pre = dot(from_table, table[...]) + met
                if pending:
                    scatter()
                pending.append((row, reach, silu(pre).astype(BF16)))
        scatter()

    for index, table in parts:
        origin = plan_ref[index, 0] // 128 * 128

        def general(block, carry):
            keys = key_ref[:, pl.ds(pl.multiple_of(origin + block * EDGES, 128), EDGES)]
            column = as_column(keys)
            receiver = lax.div(column, half) - index * mesh_rows
            from_table = one_hot((column & (half - 1)) == iota((EDGES, half), 1))
            from_recv = one_hot(receiver == iota((EDGES, mesh_rows), 1))
            message = silu(dot(from_table, table[...]) + dot(from_recv, recv_ref[:mesh_rows, :]))
            line = lax.div(keys, half) - index * mesh_rows
            line = jnp.where((keys < 0) | (line < 0) | (line >= mesh_rows), -mesh_rows, line)
            selector = one_hot(line == iota((mesh_rows, EDGES), 0))
            acc_ref[:mesh_rows, :] += dot(selector, message.astype(BF16))
            return carry

        blocks = (plan_ref[index, 1] - origin + EDGES - 1) // EDGES
        lax.fori_loop(0, jnp.where(narrow, 0, blocks), general, 0)


def high_kernel(
    low_ref,
    send_low_ref,
    msg_ref,
    line_ref,
    self_ref,
    weight_ref,
    high_ref,
    send_high_ref,
    table_ref,
    recv_ref,
    own_ref,
):
    early, width = low_ref.shape
    late = high_ref.shape[0]
    mesh_rows = early + late
    codes = receiver_code(iota((late, msg_ref.shape[0]), 0) + early).astype(F32)
    sums = dot(one_hot(line_ref[0:1, :] == codes), msg_ref[...])
    mesh = part(weight_ref, 5)[early:, :]
    high_ref[...] = next_rows(sums, self_ref[early:, :], mesh, part(weight_ref, 4)[...])
    send_high_ref[...] = dot(high_ref[...], part(weight_ref, 0)[...]).astype(BF16)
    table_ref[:early, :] = send_low_ref[...]
    table_ref[early:, :] = send_high_ref[...]
    recv_ref[mesh_rows:, :] = jnp.zeros((SPAN, width), BF16)
    for start, mid_ref in ((0, low_ref), (early, high_ref)):
        here = slice(start, start + mid_ref.shape[0])
        mid = mid_ref[...]
        recv_ref[here, :] = dot(mid, part(weight_ref, 1)[...]).astype(BF16)
        own_ref[here, :] = dot(mid, part(weight_ref, 2)[...])


def own_kernel(plan_ref, key_ref, line_ref, column_ref, table_ref, recv_ref, acc_ref):
    half = table_ref.shape[0] // 2
    acc_ref[...] = jnp.zeros_like(acc_ref)
    parts = [(0, table_ref.at[:half, :]), (1, table_ref.at[half:, :])]
    edge_sums(parts, (plan_ref, key_ref, line_ref, column_ref), recv_ref, acc_ref)


def near_kernel(
    plan_ref,
    acc_in_ref,
    key_ref,
    line_ref,
    column_ref,
    right_ref,
    left_ref,
    recv_ref,
    acc_ref,
    met_ref,
):
    parts = [(2, right_ref), (3, left_ref)]
    edge_sums(parts, (plan_ref, key_ref, line_ref, column_ref), recv_ref, acc_ref)

    @pl.when(all_narrow(plan_ref, (4, 5)))
    def _():
        for order, index in enumerate((4, 5)):
            for block in range(BLOCKS):
                at = (order * BLOCKS + block) * EDGES
                met = pick_receivers(index, block, plan_ref, column_ref, recv_ref)
                met_ref[at : at + EDGES, :] = met


def far_kernel(
    plan_ref,
    acc_in_ref,
    key_ref,
    line_ref,
    column_ref,
    right_ref,
    left_ref,
    weight_ref,
    recv_ref,
    met_ref,
    low_ref,
    high_ref,
    own_ref,
    out_hbm,
    acc_ref,
    out_ref,
    sems,
):
    early = low_ref.shape[0]
    mesh_rows = early + high_ref.shape[0]
    parts = [(4, right_ref), (5, left_ref)]
    edge_sums(parts, (plan_ref, key_ref, line_ref, column_ref), recv_ref, acc_ref, met_ref)
    copies = []
    rows = mesh_rows // sems.shape[0]
    for index in range(sems.shape[0]):
        start = index * rows
        here = slice(start, start + rows)
        update = own_ref[here, :] + dot(acc_ref[here, :].astype(BF16), part(weight_ref, 3)[...])
        mid = low_ref[here, :] if start < early else high_ref[start - early : start - early + rows, :]
        values = mid.astype(F32) + silu(update)
        mean = jnp.mean(values, axis=-1, keepdims=True)
        centered = values - mean
        variance = jnp.mean(centered * centered, axis=-1, keepdims=True)
        out_ref[here, :] = centered * lax.rsqrt(variance + 1e-05)
        copies += start_copies([(out_ref.at[here, :], out_hbm.at[here, :])], sems.at[index : index + 1])
    for copy in copies:
        copy.wait()


def body(
    grid_feat,
    mesh_nodes,
    g2m_sender,
    g2m_receiver,
    send_counts,
    edge_sender,
    edge_receiver,
    embed_in,
    embed_out,
    proj_grid,
    proj_mesh,
    node_self,
    node_agg,
    edge_send,
    edge_recv,
    out_self,
    out_agg,
):
    owners = lax.axis_size(("band", "face"))
    faces = lax.axis_size("face")
    slots = g2m_sender.shape[1]
    grid_rows, feats = grid_feat.shape
    edges = edge_sender.shape[1]
    mesh_rows, width = mesh_nodes.shape
    half = mesh_rows // 2
    there = pl.BlockSpec(memory_space=pltpu.HBM)
    dma = pltpu.SemaphoreType.DMA
    weight = pltpu.VMEM((width, width), BF16)
    rows = pltpu.VMEM((mesh_rows, width), BF16)
    rows_half = pltpu.VMEM((half, width), BF16)
    lines = pltpu.VMEM((PARTS * BLOCKS + -PARTS * BLOCKS % 8, EDGES), I32)
    columns = pltpu.VMEM((EDGES, 2 * lines.shape[0]), I32)
    rows_wide = pltpu.VMEM((mesh_rows, width), F32)
    sums = pltpu.VMEM((mesh_rows + SPAN, width), F32)

    packed, keys = call(
        functools.partial(pack_kernel, mesh_rows),
        (jax.ShapeDtypeStruct((slots, WIDE), BF16), jax.ShapeDtypeStruct((1, edges), I32)),
        (grid_feat.T, g2m_sender, g2m_receiver, send_counts, edge_sender, edge_receiver),
        (),
        scratch=[
            pltpu.VMEM((feats, grid_rows), BF16),
            pltpu.VMEM((1, slots), I32),
            pltpu.VMEM((1, slots), I32),
            pltpu.VMEM((1, owners), I32),
            pltpu.VMEM((1, edges), I32),
            pltpu.VMEM((1, edges), I32),
            pltpu.VMEM((slots, 8), I32),
            pltpu.VMEM((WIDE, grid_rows), BF16),
            pltpu.VMEM((slots, WIDE), BF16),
            pltpu.VMEM((1, edges), I32),
            dma((5,)),
            dma((1,)),
            dma((slots // SLOTS,)),
            dma,
        ],
        out_specs=(there, there),
    )
    keys = lax.sort(keys.reshape(edges), is_stable=False).reshape(1, edges)
    arrived = lax.all_to_all(
        packed.reshape(owners, slots // owners, WIDE),
        ("band", "face"),
        split_axis=0,
        concat_axis=0,
        tiled=True,
    ).reshape(slots, WIDE)
    fold, proj, own, keys, line, column, plan = call(
        weights_kernel,
        (
            weight,
            rows,
            rows_wide,
            pltpu.VMEM((1, edges + 2 * EDGES), I32),
            lines,
            columns,
            jax.ShapeDtypeStruct((PARTS, 3 + BLOCKS), I32),
        ),
        (embed_out, proj_grid, mesh_nodes, proj_mesh, node_self, keys),
        (),
        scratch=[weight] * 2 + [rows] + [weight] * 2 + [lines, pltpu.SMEM((1, edges), I32), dma((7,))],
        out_specs=[pl.BlockSpec(memory_space=pltpu.VMEM)] * 6 + [pl.BlockSpec(memory_space=pltpu.SMEM)],
    )
    embed = jnp.pad(embed_in, ((0, WIDE - feats), (0, 0)))
    low, send_low, messages, target, weights = call(
        functools.partial(gather_kernel, feats),
        (
            rows_half,
            rows_half,
            pltpu.VMEM((slots, width), BF16),
            pltpu.VMEM((8, slots), F32),
            pltpu.VMEM((6 * width, width), BF16),
        ),
        (mesh_nodes, node_agg, edge_send, edge_recv, out_self, out_agg),
        (arrived, embed, fold, proj, own),
        scratch=[pltpu.VMEM((half, width), F32), dma((6,))],
    )

    forward = [(i, (i + 1) % faces) for i in range(faces)]
    backward = [(target, source) for source, target in forward]

    def neighbours(rows):
        return lax.ppermute(rows, "face", backward), lax.ppermute(rows, "face", forward)

    near = neighbours(send_low)
    high, send_high, own_table, recv, own = call(
        high_kernel,
        (rows_half, rows_half, rows, pltpu.VMEM((mesh_rows + SPAN, width), BF16), rows_wide),
        (),
        (low, send_low, messages, target, own, weights),
    )
    far = neighbours(send_high)
    acc = call(own_kernel, sums, (), (keys, line, column, own_table, recv), smem=(plan,))
    acc, met = call(
        near_kernel,
        (sums, pltpu.VMEM((2 * BLOCKS * EDGES, width), F32)),
        (),
        (acc, keys, line, column, *near, recv),
        smem=(plan,),
        aliases={1: 0},
    )
    out, _ = call(
        far_kernel,
        (jax.ShapeDtypeStruct((mesh_rows, width), F32), sums),
        (),
        (acc, keys, line, column, *far, weights, recv, met, low, high, own),
        scratch=[rows_wide, dma((4,))],
        out_specs=(there, pl.BlockSpec(memory_space=pltpu.VMEM)),
        smem=(plan,),
        aliases={1: 1},
    )
    return out


def solution(mesh):
    split = P(("band", "face"), None)
    return jax.shard_map(
        body,
        mesh=mesh,
        in_specs=(split,) * 7 + (P(),) * 10,
        out_specs=split,
        check_vma=False,
    )
```

```python
import functools

import jax
import jax.numpy as jnp
from jax import lax
from jax.experimental import pallas as pl
from jax.experimental.pallas import tpu as pltpu
from jax.sharding import PartitionSpec as P

BF16 = jnp.bfloat16
F32 = jnp.float32
I32 = jnp.int32
WIDE = 256
DEAD = 1024
SLOTS = 2048
ARRIVED = 1024
PARTS = 6
BLOCKS = 3
EDGES = 256
SPAN = 256
ALIGN = 16
VMEM_BYTES = 40 * 1024 * 1024


def dot(a, b):
    return jnp.dot(a, b, preferred_element_type=F32)


def dot_rows(a, b):
    return lax.dot_general(a, b, (((1,), (1,)), ((), ())), preferred_element_type=F32)


def silu(v):
    half = 0.5 * v
    return half + half * jnp.tanh(half)


def one_hot(hit):
    return jnp.where(hit, 1.0, 0.0).astype(BF16)


def iota(shape, dim):
    return lax.broadcasted_iota(I32, shape, dim)


def receiver_code(receiver):
    return jnp.where(receiver <= DEAD // 4, receiver, DEAD // 4 - receiver)


def as_column(row):
    return jnp.broadcast_to(row, (8, row.shape[1])).T[:, 0:1]


def part(ref, index):
    rows = ref.shape[1]
    return ref.at[index * rows : (index + 1) * rows, :]


def start_copies(pairs, sems):
    copies = [
        pltpu.make_async_copy(source, target, sems.at[i]) for i, (source, target) in enumerate(pairs)
    ]
    for copy in copies:
        copy.start()
    return copies


def call(kernel, outs, hbm, vmem, scratch=(), out_specs=None, smem=(), aliases=None):
    def spec(space):
        return pl.BlockSpec(memory_space=space)

    if out_specs is None:
        out_specs = jax.tree.map(lambda _: spec(pltpu.VMEM), outs)
    args = list(smem)
    args += [pltpu.with_memory_space_constraint(arg, pltpu.HBM) for arg in hbm]
    args += [pltpu.with_memory_space_constraint(arg, pltpu.VMEM) for arg in vmem]
    spaces = [pltpu.SMEM] * len(smem) + [pltpu.HBM] * len(hbm) + [pltpu.VMEM] * len(vmem)
    return pl.pallas_call(
        kernel,
        out_shape=outs,
        in_specs=[spec(space) for space in spaces],
        out_specs=out_specs,
        scratch_shapes=list(scratch),
        input_output_aliases=aliases or {},
        compiler_params=pltpu.CompilerParams(vmem_limit_bytes=VMEM_BYTES),
    )(*args)


def pack_kernel(
    mesh_rows,
    feat_hbm,
    sender_hbm,
    receiver_hbm,
    count_hbm,
    from_hbm,
    to_hbm,
    out_hbm,
    key_hbm,
    feat_ref,
    sender_ref,
    receiver_ref,
    count_ref,
    from_ref,
    to_ref,
    column_ref,
    pad_ref,
    out_ref,
    key_ref,
    in_sem,
    feat_sem,
    out_sem,
    key_sem,
):
    feats, rows = feat_ref.shape
    slots = sender_ref.shape[1]
    owners = count_ref.shape[1]
    cap = slots // owners
    half = mesh_rows // 2
    small = start_copies(
        (
            (sender_hbm, sender_ref),
            (receiver_hbm, receiver_ref),
            (count_hbm, count_ref),
            (from_hbm, from_ref),
            (to_hbm, to_ref),
        ),
        in_sem,
    )
    pieces = feat_sem.shape[0]
    piece = rows // pieces
    cuts = [slice(i * piece, (i + 1) * piece) for i in range(pieces)]
    large = start_copies([(feat_hbm.at[:, cut], feat_ref.at[:, cut]) for cut in cuts], feat_sem)
    for copy in small:
        copy.wait()
    source = from_ref[...]
    row = lax.rem(source, mesh_rows)
    second = row // half
    mine = (source >= mesh_rows) & (source < 2 * mesh_rows)
    left = (source < mesh_rows).astype(I32)
    part = jnp.where(mine, second, 2 + 2 * second + left)
    place = row - second * half
    key_ref[...] = (part * mesh_rows + to_ref[...]) * half + place
    key_copy = pltpu.make_async_copy(key_ref, key_hbm, key_sem)
    key_copy.start()
    counts = jnp.broadcast_to(count_ref[...].astype(F32).astype(BF16), (8, owners))
    slot = iota((owners, slots), 1)
    first = iota((owners, slots), 0) * cap
    count = dot(counts, one_hot((slot >= first) & (slot < first + cap))).astype(I32)
    live = lax.rem(iota((8, slots), 1), cap) < count
    receiver = jnp.broadcast_to(receiver_ref[...], (8, slots))
    sender = jnp.broadcast_to(sender_ref[...], (8, slots))
    code = jnp.where(live, receiver_code(receiver), DEAD)
    column_ref[...] = jnp.where(iota((8, slots), 0) == 0, sender, code).T
    for copy in large:
        copy.wait()
    whole = feats // ALIGN * ALIGN
    pad_ref[:whole, :] = feat_ref[:whole, :]
    line = iota((WIDE - whole, rows), 0)
    rest = jnp.zeros((WIDE - whole, rows), F32)
    for i in range(whole, feats):
        rest = jnp.where(line == i - whole, feat_ref[i : i + 1, :].astype(F32), rest)
    pad_ref[whole:, :] = rest.astype(BF16)

    def leave(block):
        here = pl.ds(pl.multiple_of(block * SLOTS, SLOTS), SLOTS)
        return pltpu.make_async_copy(out_ref.at[here, :], out_hbm.at[here, :], out_sem.at[block])

    def step(block, carry):
        start = pl.multiple_of(block * SLOTS, SLOTS)
        here = pl.ds(start, SLOTS)
        columns = column_ref[here, :]
        picker = one_hot(columns[:, 0:1] == iota((SLOTS, rows), 1))
        column = iota((SLOTS, WIDE), 1)
        code = jnp.where(column == feats, columns[:, 1:2], 0).astype(F32)
        out_ref[here, :] = (dot_rows(picker, pad_ref[...]) + code).astype(BF16)
        leave(block).start()
        return carry

    lax.fori_loop(0, slots // SLOTS, step, 0)
    for block in range(slots // SLOTS):
        leave(block).wait()
    key_copy.wait()


def weights_kernel(
    embed_out_hbm,
    proj_grid_hbm,
    mesh_hbm,
    proj_mesh_hbm,
    node_self_hbm,
    key_hbm,
    fold_ref,
    proj_ref,
    self_ref,
    key_ref,
    line_ref,
    column_ref,
    plan_ref,
    embed_out_ref,
    proj_grid_ref,
    mesh_ref,
    proj_mesh_ref,
    node_self_ref,
    place_ref,
    key_scalar,
    sems,
):
    edges = key_hbm.shape[1]
    pairs = (
        (embed_out_hbm, embed_out_ref),
        (proj_grid_hbm, proj_grid_ref),
        (mesh_hbm, mesh_ref),
        (proj_mesh_hbm, proj_mesh_ref),
        (node_self_hbm, node_self_ref),
        (key_hbm, key_ref.at[:, :edges]),
        (key_hbm, key_scalar),
    )
    copies = start_copies(pairs, sems)
    key_ref[:, edges:] = jnp.full((1, key_ref.shape[1] - edges), -1, I32)
    for copy in copies:
        copy.wait()
    plan_edges(key_scalar, key_ref, plan_ref, line_ref, place_ref, column_ref, mesh_ref.shape[0])
    fold_ref[...] = dot(embed_out_ref[...], proj_grid_ref[...]).astype(BF16)
    mesh = mesh_ref[...]
    proj_ref[...] = dot(mesh, proj_mesh_ref[...]).astype(BF16)
    self_ref[...] = dot(mesh, node_self_ref[...])


def next_rows(sums, own, mesh, node_agg):
    inner = own + dot(sums.astype(BF16), node_agg)
    return (mesh.astype(F32) + silu(inner)).astype(BF16)


def gather_kernel(
    feats,
    mesh_hbm,
    node_agg_hbm,
    edge_send_hbm,
    edge_recv_hbm,
    out_self_hbm,
    out_agg_hbm,
    x_ref,
    embed_ref,
    fold_ref,
    proj_ref,
    self_ref,
    low_ref,
    send_ref,
    msg_ref,
    line_ref,
    weight_ref,
    sum_ref,
    sems,
):
    sources = (edge_send_hbm, edge_recv_hbm, out_self_hbm, out_agg_hbm, node_agg_hbm, mesh_hbm)
    copies = start_copies([(hbm, part(weight_ref, i)) for i, hbm in enumerate(sources)], sems)
    slots = x_ref.shape[0]
    mesh_rows = self_ref.shape[0]
    early = low_ref.shape[0]
    lanes = feats // 128 * 128
    along = one_hot(iota((8, WIDE - lanes), 1) == feats - lanes)
    sum_ref[...] = jnp.zeros_like(sum_ref)

    def step(block, carry):
        here = pl.ds(pl.multiple_of(block * ARRIVED, ARRIVED), ARRIVED)
        x = x_ref[here, :]
        hidden = silu(dot(x, embed_ref[...])).astype(BF16)
        column = x[:, feats : feats + 1].astype(F32)
        codes = receiver_code(iota((ARRIVED, mesh_rows), 1)).astype(F32)
        picker = one_hot(column == codes)
        message = silu(dot(hidden, fold_ref[...]) + dot(picker, proj_ref[...])).astype(BF16)
        msg_ref[here, :] = message
        line = dot_rows(along, x[:, lanes:])
        line_ref[:, here] = line
        codes = receiver_code(iota((early, ARRIVED), 0)).astype(F32)
        sum_ref[...] += dot(one_hot(line[0:1, :] == codes), message)
        return carry

    lax.fori_loop(0, slots // ARRIVED, step, 0)
    for copy in copies:
        copy.wait()
    mesh = part(weight_ref, 5)[:early, :]
    low_ref[...] = next_rows(sum_ref[...], self_ref[:early, :], mesh, part(weight_ref, 4)[...])
    send_ref[...] = dot(low_ref[...], part(weight_ref, 0)[...]).astype(BF16)


def plan_edges(key_scalar, key_ref, plan_ref, line_ref, place_ref, column_ref, mesh_rows):
    edges = key_scalar.shape[1]
    half = mesh_rows // 2

    def first_at_least(limit):
        def halve(_, ends):
            low, high = ends
            middle = (low + high) // 2
            below = key_scalar[0, jnp.minimum(middle, edges - 1)] < limit
            go = low < high
            return (
                jnp.where(go & below, middle + 1, low),
                jnp.where(go & jnp.logical_not(below), middle, high),
            )

        ends = (jnp.int32(0), jnp.int32(edges))
        return lax.fori_loop(0, edges.bit_length(), halve, ends)[0]

    first = jnp.int32(0)
    lines = []
    places = []
    for index in range(PARTS):
        last = jnp.int32(edges)
        if index < PARTS - 1:
            last = first_at_least((index + 1) * mesh_rows * half)
        share = jnp.minimum((last - first + BLOCKS - 1) // BLOCKS, EDGES)

        def receiver_at(position):
            key = key_scalar[0, jnp.clip(position, 0, edges - 1)]
            return key // half - index * mesh_rows

        narrow = jnp.bool_(True)
        for block in range(BLOCKS):
            start = jnp.minimum(first + block * share, last)
            end = jnp.minimum(start + share, last)
            empty = start >= end
            base = jnp.where(empty, 0, receiver_at(start) // ALIGN * ALIGN)
            narrow = narrow & (empty | (receiver_at(end - 1) - base < SPAN))
            plan_ref[index, 3 + block] = base
            begin = pl.multiple_of(start // 128 * 128, 128)
            width = EDGES + 128
            keys = jnp.broadcast_to(key_ref[:, pl.ds(begin, width)], (8, width))
            keys = pltpu.roll(keys, lax.rem(width - (start - begin), width), axis=1)[0:1, :EDGES]
            live = iota((1, EDGES), 1) < end - start
            receiver = lax.div(keys, half) - index * mesh_rows - base
            lines.append(jnp.where(live, receiver, -mesh_rows))
            places.append(keys & (half - 1))
        plan_ref[index, 0] = first
        plan_ref[index, 1] = last
        plan_ref[index, 2] = narrow.astype(I32)
        plan_ref[index, 3 + BLOCKS] = jnp.minimum(first + BLOCKS * share, last)
        first = last
    rows = line_ref.shape[0]
    for block in range(PARTS * BLOCKS):
        line_ref[block : block + 1, :] = lines[block]
        place_ref[block : block + 1, :] = places[block]
    for block in range(PARTS * BLOCKS, rows):
        line_ref[block : block + 1, :] = jnp.full((1, EDGES), -mesh_rows, I32)
        place_ref[block : block + 1, :] = jnp.zeros((1, EDGES), I32)
    column_ref[:, :rows] = line_ref[...].T
    column_ref[:, rows:] = place_ref[...].T


def all_narrow(plan_ref, indices):
    return functools.reduce(jnp.logical_and, [plan_ref[index, 2] == 1 for index in indices])


def reach_of(plan_ref, index, block):
    return pl.ds(pl.multiple_of(plan_ref[index, 3 + block], ALIGN), SPAN)


def pick_receivers(index, block, plan_ref, column_ref, recv_ref):
    row = index * BLOCKS + block
    picker = one_hot(column_ref[:, row : row + 1] == iota((EDGES, SPAN), 1))
    return dot(picker, recv_ref[reach_of(plan_ref, index, block), :])


def edge_sums(parts, plan_refs, recv_ref, acc_ref, met_ref=None):
    plan_ref, key_ref, line_ref, column_ref = plan_refs
    half = parts[0][1].shape[0]
    mesh_rows = 2 * half
    rows = line_ref.shape[0]
    narrow = all_narrow(plan_ref, [index for index, _ in parts])

    @pl.when(narrow)
    def _():
        pending = []

        def scatter():
            row, reach, message = pending.pop(0)
            selector = one_hot(line_ref[row : row + 1, :] == iota((SPAN, EDGES), 0))
            acc_ref[reach, :] += dot(selector, message)

        for order, (index, table) in enumerate(parts):
            for block in range(BLOCKS):
                row = index * BLOCKS + block
                reach = reach_of(plan_ref, index, block)
                place = column_ref[:, rows + row : rows + row + 1]
                from_table = one_hot(place == iota((EDGES, half), 1))
                if met_ref is None:
                    met = pick_receivers(index, block, plan_ref, column_ref, recv_ref)
                else:
                    at = (order * BLOCKS + block) * EDGES
                    met = met_ref[at : at + EDGES, :]
                pre = dot(from_table, table[...]) + met
                if pending:
                    scatter()
                pending.append((row, reach, silu(pre).astype(BF16)))
        scatter()

    for index, table in parts:
        first = jnp.where(narrow, plan_ref[index, 3 + BLOCKS], plan_ref[index, 0])
        last = plan_ref[index, 1]
        origin = first // 128 * 128

        def general(block, carry, index=index, table=table, first=first, last=last, origin=origin):
            start = pl.multiple_of(origin + block * EDGES, 128)
            keys = key_ref[:, pl.ds(start, EDGES)]
            column = as_column(keys)
            receiver = lax.div(column, half) - index * mesh_rows
            from_table = one_hot((column & (half - 1)) == iota((EDGES, half), 1))
            from_recv = one_hot(receiver == iota((EDGES, mesh_rows), 1))
            message = silu(dot(from_table, table[...]) + dot(from_recv, recv_ref[:mesh_rows, :]))
            line = lax.div(keys, half) - index * mesh_rows
            place = iota((1, EDGES), 1) + start
            line = jnp.where((place >= first) & (place < last), line, -mesh_rows)
            selector = one_hot(line == iota((mesh_rows, EDGES), 0))
            acc_ref[:mesh_rows, :] += dot(selector, message.astype(BF16))
            return carry

        blocks = (last - origin + EDGES - 1) // EDGES
        lax.fori_loop(0, jnp.where(first < last, blocks, 0), general, 0)


def high_kernel(
    low_ref,
    send_low_ref,
    msg_ref,
    line_ref,
    self_ref,
    weight_ref,
    high_ref,
    send_high_ref,
    table_ref,
    recv_ref,
    own_ref,
):
    early, width = low_ref.shape
    late = high_ref.shape[0]
    mesh_rows = early + late
    codes = receiver_code(iota((late, msg_ref.shape[0]), 0) + early).astype(F32)
    sums = dot(one_hot(line_ref[0:1, :] == codes), msg_ref[...])
    mesh = part(weight_ref, 5)[early:, :]
    high_ref[...] = next_rows(sums, self_ref[early:, :], mesh, part(weight_ref, 4)[...])
    send_high_ref[...] = dot(high_ref[...], part(weight_ref, 0)[...]).astype(BF16)
    table_ref[:early, :] = send_low_ref[...]
    table_ref[early:, :] = send_high_ref[...]
    recv_ref[mesh_rows:, :] = jnp.zeros((SPAN, width), BF16)
    for start, mid_ref in ((0, low_ref), (early, high_ref)):
        here = slice(start, start + mid_ref.shape[0])
        mid = mid_ref[...]
        recv_ref[here, :] = dot(mid, part(weight_ref, 1)[...]).astype(BF16)
        own_ref[here, :] = dot(mid, part(weight_ref, 2)[...])


def own_kernel(plan_ref, key_ref, line_ref, column_ref, table_ref, recv_ref, acc_ref):
    half = table_ref.shape[0] // 2
    acc_ref[...] = jnp.zeros_like(acc_ref)
    parts = [(0, table_ref.at[:half, :]), (1, table_ref.at[half:, :])]
    edge_sums(parts, (plan_ref, key_ref, line_ref, column_ref), recv_ref, acc_ref)


def near_kernel(
    plan_ref,
    acc_in_ref,
    key_ref,
    line_ref,
    column_ref,
    right_ref,
    left_ref,
    recv_ref,
    acc_ref,
    met_ref,
):
    parts = [(2, right_ref), (3, left_ref)]
    edge_sums(parts, (plan_ref, key_ref, line_ref, column_ref), recv_ref, acc_ref)

    @pl.when(all_narrow(plan_ref, (4, 5)))
    def _():
        for order, index in enumerate((4, 5)):
            for block in range(BLOCKS):
                at = (order * BLOCKS + block) * EDGES
                met = pick_receivers(index, block, plan_ref, column_ref, recv_ref)
                met_ref[at : at + EDGES, :] = met


def far_kernel(
    plan_ref,
    acc_in_ref,
    key_ref,
    line_ref,
    column_ref,
    right_ref,
    left_ref,
    weight_ref,
    recv_ref,
    met_ref,
    low_ref,
    high_ref,
    own_ref,
    out_hbm,
    acc_ref,
    out_ref,
    sems,
):
    early = low_ref.shape[0]
    mesh_rows = early + high_ref.shape[0]
    parts = [(4, right_ref), (5, left_ref)]
    edge_sums(parts, (plan_ref, key_ref, line_ref, column_ref), recv_ref, acc_ref, met_ref)
    copies = []
    rows = mesh_rows // sems.shape[0]
    for index in range(sems.shape[0]):
        start = index * rows
        here = slice(start, start + rows)
        update = own_ref[here, :] + dot(acc_ref[here, :].astype(BF16), part(weight_ref, 3)[...])
        mid = low_ref[here, :] if start < early else high_ref[start - early : start - early + rows, :]
        values = mid.astype(F32) + silu(update)
        mean = jnp.mean(values, axis=-1, keepdims=True)
        centered = values - mean
        variance = jnp.mean(centered * centered, axis=-1, keepdims=True)
        out_ref[here, :] = centered * lax.rsqrt(variance + 1e-05)
        copies += start_copies([(out_ref.at[here, :], out_hbm.at[here, :])], sems.at[index : index + 1])
    for copy in copies:
        copy.wait()


def body(
    grid_feat,
    mesh_nodes,
    g2m_sender,
    g2m_receiver,
    send_counts,
    edge_sender,
    edge_receiver,
    embed_in,
    embed_out,
    proj_grid,
    proj_mesh,
    node_self,
    node_agg,
    edge_send,
    edge_recv,
    out_self,
    out_agg,
):
    owners = lax.axis_size(("band", "face"))
    faces = lax.axis_size("face")
    slots = g2m_sender.shape[1]
    grid_rows, feats = grid_feat.shape
    edges = edge_sender.shape[1]
    mesh_rows, width = mesh_nodes.shape
    half = mesh_rows // 2
    there = pl.BlockSpec(memory_space=pltpu.HBM)
    dma = pltpu.SemaphoreType.DMA
    weight = pltpu.VMEM((width, width), BF16)
    rows = pltpu.VMEM((mesh_rows, width), BF16)
    rows_half = pltpu.VMEM((half, width), BF16)
    lines = pltpu.VMEM((PARTS * BLOCKS + -PARTS * BLOCKS % 8, EDGES), I32)
    columns = pltpu.VMEM((EDGES, 2 * lines.shape[0]), I32)
    rows_wide = pltpu.VMEM((mesh_rows, width), F32)
    sums = pltpu.VMEM((mesh_rows + SPAN, width), F32)

    packed, keys = call(
        functools.partial(pack_kernel, mesh_rows),
        (jax.ShapeDtypeStruct((slots, WIDE), BF16), jax.ShapeDtypeStruct((1, edges), I32)),
        (grid_feat.T, g2m_sender, g2m_receiver, send_counts, edge_sender, edge_receiver),
        (),
        scratch=[
            pltpu.VMEM((feats, grid_rows), BF16),
            pltpu.VMEM((1, slots), I32),
            pltpu.VMEM((1, slots), I32),
            pltpu.VMEM((1, owners), I32),
            pltpu.VMEM((1, edges), I32),
            pltpu.VMEM((1, edges), I32),
            pltpu.VMEM((slots, 8), I32),
            pltpu.VMEM((WIDE, grid_rows), BF16),
            pltpu.VMEM((slots, WIDE), BF16),
            pltpu.VMEM((1, edges), I32),
            dma((5,)),
            dma((1,)),
            dma((slots // SLOTS,)),
            dma,
        ],
        out_specs=(there, there),
    )
    keys = lax.sort(keys.reshape(edges), is_stable=False).reshape(1, edges)
    arrived = lax.all_to_all(
        packed.reshape(owners, slots // owners, WIDE),
        ("band", "face"),
        split_axis=0,
        concat_axis=0,
        tiled=True,
    ).reshape(slots, WIDE)
    fold, proj, own, keys, line, column, plan = call(
        weights_kernel,
        (
            weight,
            rows,
            rows_wide,
            pltpu.VMEM((1, edges + 2 * EDGES), I32),
            lines,
            columns,
            jax.ShapeDtypeStruct((PARTS, 4 + BLOCKS), I32),
        ),
        (embed_out, proj_grid, mesh_nodes, proj_mesh, node_self, keys),
        (),
        scratch=[weight] * 2 + [rows] + [weight] * 2 + [lines, pltpu.SMEM((1, edges), I32), dma((7,))],
        out_specs=[pl.BlockSpec(memory_space=pltpu.VMEM)] * 6 + [pl.BlockSpec(memory_space=pltpu.SMEM)],
    )
    embed = jnp.pad(embed_in, ((0, WIDE - feats), (0, 0)))
    low, send_low, messages, target, weights = call(
        functools.partial(gather_kernel, feats),
        (
            rows_half,
            rows_half,
            pltpu.VMEM((slots, width), BF16),
            pltpu.VMEM((8, slots), F32),
            pltpu.VMEM((6 * width, width), BF16),
        ),
        (mesh_nodes, node_agg, edge_send, edge_recv, out_self, out_agg),
        (arrived, embed, fold, proj, own),
        scratch=[pltpu.VMEM((half, width), F32), dma((6,))],
    )

    forward = [(i, (i + 1) % faces) for i in range(faces)]
    backward = [(target, source) for source, target in forward]

    def neighbours(rows):
        return lax.ppermute(rows, "face", backward), lax.ppermute(rows, "face", forward)

    near = neighbours(send_low)
    high, send_high, own_table, recv, own = call(
        high_kernel,
        (rows_half, rows_half, rows, pltpu.VMEM((mesh_rows + SPAN, width), BF16), rows_wide),
        (),
        (low, send_low, messages, target, own, weights),
    )
    far = neighbours(send_high)
    acc = call(own_kernel, sums, (), (keys, line, column, own_table, recv), smem=(plan,))
    acc, met = call(
        near_kernel,
        (sums, pltpu.VMEM((2 * BLOCKS * EDGES, width), F32)),
        (),
        (acc, keys, line, column, *near, recv),
        smem=(plan,),
        aliases={1: 0},
    )
    out, _ = call(
        far_kernel,
        (jax.ShapeDtypeStruct((mesh_rows, width), F32), sums),
        (),
        (acc, keys, line, column, *far, weights, recv, met, low, high, own),
        scratch=[rows_wide, dma((4,))],
        out_specs=(there, pl.BlockSpec(memory_space=pltpu.VMEM)),
        smem=(plan,),
        aliases={1: 1},
    )
    return out


def solution(mesh):
    split = P(("band", "face"), None)
    return jax.shard_map(
        body,
        mesh=mesh,
        in_specs=(split,) * 7 + (P(),) * 10,
        out_specs=split,
        check_vma=False,
    )
```
